32 devices in a mesh: grp: 2 (over y), seq: 4 (over z), head: 2 (over x), hold: 2 (over core).
Axes of the slice: x: 2, y: 2, z: 4, core: 2. Of those that a mesh axis runs over, the one named last changes fastest.
Arguments:
- meet_span: int32 [2], P('grp'), parts along dimension 0, may hold values from 2 to 6
- span_map: int32 [16], P('grp'), parts along dimension 0, may hold values from 0 to 7, each once
- hidden: bfloat16 [4096, 8192], P(('grp', 'seq')), parts along dimension 0, may hold values from -6 to 6
- w_query: bfloat16 [8192, 8, 512], P('seq', ('head', 'hold')), may hold values from -0.0625 to 0.0625
- w_keyval: bfloat16 [8192, 8, 256], P('seq', ('head', 'hold')), may hold values from -0.0625 to 0.0625
- stored_kv: bfloat16 [4096, 8, 256], P(('grp', 'seq'), ('head', 'hold')), parts along dimension 0, may hold values from -650 to 650, as said below
Outputs:
- attended: bfloat16 [4096, 8, 512], P(('grp', 'seq'), ('head', 'hold')), parts along dimension 0
- kv_cache: bfloat16 [4096, 8, 256], P(('grp', 'seq'), ('head', 'hold')), parts along dimension 0
The draws below stay inside these ranges and needn't reach their ends.
There are 2 independent parts, one for each index of `grp`. The reference program is written for one: setup_inputs(seed, part) draws one part's arguments, and reference() takes and returns one part's arrays. A program takes and returns all parts, laid end to end along the dimension named above; an argument that names none is the same for every part. Nothing has to cross between parts.
Inputs may be any that keep to these rules, and one draw needn't show every extreme that they name: `stored_kv`: keys may be large on some rows.
All inputs are finite; a program needn't handle non-finite values.
Results may differ from the reference program's by a relative error of at most 0.012.
Values may be sent and summed in bfloat16 or wider, within the bound.
A program may use at most 128 MiB of HBM per device.

```python
import jax
import jax.numpy as jnp
from jax import lax

D = 8192
HD = 128
KVH = 8
QPK = 4
CH = 256
NCH = 8
TOKENS = 2048


def draw_stored_kv(key, part):
    key_one = jax.random.fold_in(jax.random.fold_in(key, 7321), 0)
    base_draw = jnp.clip(jax.random.normal(key_one, (NCH * CH, KVH, 2 * HD), jnp.float32), -6.0, 6.0)
    return base_draw.astype(jnp.bfloat16)


def levels(key, dims, cuts, low, high):
    level = 1.0
    for axis_at, blocks in cuts:
        heights = jax.random.uniform(jax.random.fold_in(jax.random.fold_in(key, 6), axis_at), (blocks,), jnp.float32, low / len(cuts), high / len(cuts))
        level = level * jnp.repeat(jnp.exp(heights), dims[axis_at] // blocks).reshape((-1,) + (1,) * (len(dims) - 1 - axis_at))
    return level


def scatter_about(own_key, extent, deviation, reach, pieces=(), kind=jnp.bfloat16):
    values = deviation * jax.random.normal(own_key, extent, jnp.float32)
    if pieces:
        values = values * levels(own_key, extent, pieces, -0.22, 0.18)
    return jnp.clip(values, -reach, reach).astype(kind)


def setup_inputs(seed: int = 0, part: int = 0) -> dict:
    seeds = jax.random.split(jax.random.key(seed), 7)
    part_splits = jax.random.split(jax.random.fold_in(seeds[6], part), 7)
    meet_span = jax.random.randint(part_splits[0], (1,), NCH // 4, 3 * NCH // 4 + 1).astype(jnp.int32)
    span_map = jax.random.permutation(part_splits[1], NCH).astype(jnp.int32)
    hidden = scatter_about(part_splits[2], (TOKENS, D), 1.0, 6.0, ((0, 4),))
    w_query = scatter_about(seeds[3], (D, KVH, QPK * HD), D ** -0.5, 0.0625, ((0, 4), (1, 4)))
    w_keyval = scatter_about(seeds[4], (D, KVH, 2 * HD), D ** -0.5, 0.0625, ((0, 4), (1, 4)))
    stored_kv = draw_stored_kv(jax.random.fold_in(jax.random.fold_in(seeds[6], part), 71), part)
    return dict(meet_span=meet_span, span_map=span_map, hidden=hidden, w_query=w_query, w_keyval=w_keyval, stored_kv=stored_kv)


theta_base = 500000.0


def rotate(values, positions):
    half_width = values.shape[-1] // 2
    frequency = theta_base ** (-(jnp.arange(half_width, dtype=jnp.float32) * 2.0) / values.shape[-1])
    angles = positions.astype(jnp.float32)[:, None] * frequency[None, :]
    bcast_shape = (positions.shape[0],) + (1,) * (values.ndim - 2) + (half_width,)
    cosine = jnp.cos(angles).reshape(bcast_shape)
    sine_part = jnp.sin(angles).reshape(bcast_shape)
    lower_half = values[..., :half_width]
    upper_half = values[..., half_width:]
    return jnp.concatenate([lower_half * cosine - upper_half * sine_part, upper_half * cosine + lower_half * sine_part], -1)


def reference(meet_span, span_map, hidden, w_query, w_keyval, stored_kv):
    row_total = hidden.shape[0]
    features = hidden.shape[1]
    span_count = span_map.shape[0]
    span_len = row_total // span_count
    head_count = w_query.shape[1]
    head_width = stored_kv.shape[2] // 2
    group_size = w_query.shape[2] // head_width
    row_ids = jnp.arange(row_total, dtype=jnp.int32)
    row_span = span_map[row_ids // span_len]
    positions = (row_span * span_len + row_ids % span_len).astype(jnp.int32)
    computed = (row_span < meet_span[0]) | (row_span == span_count - 1)
    query_raw = jnp.dot(hidden, w_query.reshape(features, -1), preferred_element_type=jnp.float32)
    query_raw = query_raw.reshape(row_total, head_count, group_size, head_width)
    queries = rotate(query_raw, positions).astype(jnp.bfloat16)
    keyval_raw = jnp.dot(hidden, w_keyval.reshape(features, -1), preferred_element_type=jnp.float32)
    keyval_raw = keyval_raw.reshape(row_total, head_count, 2 * head_width)
    rotated = rotate(keyval_raw[..., :head_width], positions)
    recomputed = jnp.concatenate([rotated, keyval_raw[..., head_width:]], -1).astype(jnp.bfloat16)
    full_cache = jnp.where(computed[:, None, None], recomputed, stored_kv)
    cache_keys = full_cache[..., :head_width].astype(jnp.float32)
    cache_values = full_cache[..., head_width:].astype(jnp.float32)
    score_scale = head_width ** -0.5

    def one_span(span_index):
        span_queries = lax.dynamic_slice_in_dim(queries, span_index * span_len, span_len, 0).astype(jnp.float32)
        query_pos = lax.dynamic_slice_in_dim(positions, span_index * span_len, span_len, 0)
        scores = jnp.einsum('ckgd,nkd->kgcn', span_queries, cache_keys) * score_scale
        allowed = positions[None, None, None, :] <= query_pos[None, None, :, None]
        scores = jnp.where(allowed, scores, -jnp.inf)
        row_max = scores.max(-1, keepdims=True)
        weights = jnp.where(allowed, jnp.exp(scores - row_max), 0.0)
        numerator = jnp.einsum('kgcn,nkd->kgcd', weights.astype(jnp.bfloat16).astype(jnp.float32), cache_values)
        result = numerator / weights.sum(-1, keepdims=True)
        return jnp.transpose(result, (2, 0, 1, 3)).reshape(span_len, head_count, group_size * head_width)

    per_span = lax.map(one_span, jnp.arange(span_count, dtype=jnp.int32))
    attended = per_span.reshape(row_total, head_count, group_size * head_width)
    attended = jnp.where(computed[:, None, None], attended, 0.0).astype(jnp.bfloat16)
    return attended, full_cache
```

```python
import functools
import math

import jax
import jax.numpy as jnp
from jax import lax
from jax.experimental import pallas as pl
from jax.experimental.pallas import tpu as pltpu
from jax.sharding import PartitionSpec as P

CH = 256
MESH = pl.DeviceIdType.MESH

theta_base = 500000.0
lowest = -1e30


def rotary_tables(positions, head_width):
    half_width = head_width // 2
    frequency = theta_base ** (
        -(jnp.arange(half_width, dtype=jnp.float32) * 2.0) / head_width
    )
    angles = positions.astype(jnp.float32)[:, None] * frequency[None, :]
    cosine, sine = jnp.cos(angles), jnp.sin(angles)
    return jnp.concatenate([cosine, cosine], -1), jnp.concatenate([-sine, sine], -1)


def kernel(
    n, groups, local_heads, group_size,
    hidden_hbm, own_w, stored, cos_ref, sin_ref, qpos_ref, done_ref, kpos_ref,
    out_ref, cache_ref,
    hid, wbuf, kvbuf, qbuf, acc,
    hid_sem, own_sem, up_send, down_send, z_recv, y_send, y_recv,
    kv_up, kv_down, kv_recv,
):
    s = lax.axis_index("seq")
    g = lax.axis_index("grp")
    rows = hid.shape[0]
    chunks, depth, width = own_w.shape
    part = depth // groups
    planes = 2 * local_heads
    has_up, has_down = s + 1 < n, s > 0

    barrier = pltpu.get_barrier_semaphore()

    @pl.when(has_up)
    def _():
        pl.semaphore_signal(barrier, inc=1, device_id={"seq": s + 1}, device_id_type=MESH)

    @pl.when(has_down)
    def _():
        pl.semaphore_signal(barrier, inc=1, device_id={"seq": s - 1}, device_id_type=MESH)

    for k in range(1, groups):
        pl.semaphore_signal(
            barrier, inc=1, device_id={"grp": lax.rem(g + k, groups)}, device_id_type=MESH
        )
    hid_copy = pltpu.make_async_copy(hidden_hbm, hid, hid_sem)
    hid_copy.start()
    own_copy = pltpu.make_async_copy(
        own_w, wbuf.at[:, pl.ds(pl.multiple_of(s * depth, depth), depth), :], own_sem
    )
    own_copy.start()
    pl.semaphore_wait(
        barrier, jnp.where(has_up, 1, 0) + jnp.where(has_down, 1, 0) + (groups - 1)
    )

    def piece(c, o, gg):
        return wbuf.at[c, pl.ds(pl.multiple_of(o * depth + gg * part, part), part), :]

    def kv_piece(j, o):
        return kvbuf.at[j, pl.ds(pl.multiple_of(o * rows, rows), rows), :]

    def up_copy(c, o, src):
        return pltpu.make_async_remote_copy(
            src_ref=src, dst_ref=piece(c, o, g), send_sem=up_send.at[c, o],
            recv_sem=z_recv.at[c, o], device_id={"seq": s + 1}, device_id_type=MESH,
        )

    def down_copy(c, o, src):
        return pltpu.make_async_remote_copy(
            src_ref=src, dst_ref=piece(c, o, g), send_sem=down_send.at[c, o],
            recv_sem=z_recv.at[c, o], device_id={"seq": s - 1}, device_id_type=MESH,
        )

    def side_copy(c, o, sender, target):
        return pltpu.make_async_remote_copy(
            src_ref=piece(c, o, sender), dst_ref=piece(c, o, sender),
            send_sem=y_send.at[c, o, target], recv_sem=y_recv.at[c, o, sender],
            device_id={"grp": target}, device_id_type=MESH,
        )

    def kv_up_copy(j, o):
        return pltpu.make_async_remote_copy(
            src_ref=kv_piece(j, o), dst_ref=kv_piece(j, o), send_sem=kv_up.at[j, o],
            recv_sem=kv_recv.at[j, o], device_id={"seq": s + 1}, device_id_type=MESH,
        )

    def kv_down_copy(j, o):
        return pltpu.make_async_remote_copy(
            src_ref=kv_piece(j, o), dst_ref=kv_piece(j, o), send_sem=kv_down.at[j, o],
            recv_sem=kv_recv.at[j, o], device_id={"seq": s - 1}, device_id_type=MESH,
        )

    def send_own(c):
        src = own_w.at[c, pl.ds(pl.multiple_of(g * part, part), part), :]

        @pl.when(has_up)
        def _():
            up_copy(c, s, src).start()

        @pl.when(has_down)
        def _():
            down_copy(c, s, src).start()

    def forward(c):
        def hop(d, _):
            lo, hi = s - d, s + d

            @pl.when(lo >= 0)
            def _():
                up_copy(c, lo, piece(c, lo, g)).wait_recv()

                @pl.when(has_up)
                def _():
                    up_copy(c, lo, piece(c, lo, g)).start()

                for k in range(1, groups):
                    side_copy(c, lo, g, lax.rem(g + k, groups)).start()

            @pl.when(hi < n)
            def _():
                down_copy(c, hi, piece(c, hi, g)).wait_recv()

                @pl.when(has_down)
                def _():
                    down_copy(c, hi, piece(c, hi, g)).start()

                for k in range(1, groups):
                    side_copy(c, hi, g, lax.rem(g + k, groups)).start()

            return 0

        lax.fori_loop(1, n, hop, 0)

    def kv_hop(j, d):
        lo, hi = s - d, s + d

        @pl.when(lo >= 0)
        def _():
            kv_up_copy(j, lo).wait_recv()

            @pl.when(has_up)
            def _():
                kv_up_copy(j, lo).start()

        @pl.when(hi < n)
        def _():
            kv_down_copy(j, hi).wait_recv()

            @pl.when(has_down)
            def _():
                kv_down_copy(j, hi).start()

    def project(c):
        def gather_side(o, _):
            @pl.when(o != s)
            def _():
                for k in range(1, groups):
                    other = lax.rem(g + k, groups)
                    side_copy(c, o, other, g).wait_recv()

            return 0

        lax.fori_loop(0, n, gather_side, 0)
        acc[...] = jnp.zeros_like(acc)

        def add(o, _):
            at = pl.ds(pl.multiple_of(o * depth, depth), depth)
            acc[...] += jnp.dot(
                hid[:, at], wbuf[c, at, :], preferred_element_type=jnp.float32
            )
            return 0

        lax.fori_loop(0, n, add, 0)

    def rotated():
        raw = acc[...]
        half = width // 2
        turned = jnp.concatenate([raw[:, half:], raw[:, :half]], -1)
        return raw * cos_ref[...] + turned * sin_ref[...]

    row_block = 128
    scale = width ** (-0.5) * math.log2(math.e)

    def attend(q):
        head = q // group_size

        def block(b, _):
            at = pl.ds(pl.multiple_of(b * row_block, row_block), row_block)
            scores = lax.dot_general(
                qbuf[at, :], kvbuf[2 * head], (((1,), (1,)), ((), ())),
                preferred_element_type=jnp.float32,
            ) * scale
            scores = jnp.where(kpos_ref[...] <= qpos_ref[at, :], scores, lowest)
            top = scores.max(-1, keepdims=True)
            weights = jnp.exp2(scores - top)
            total = weights.sum(-1, keepdims=True)
            mixed = jnp.dot(
                weights.astype(jnp.bfloat16), kvbuf[2 * head + 1],
                preferred_element_type=jnp.float32,
            ) / total
            out_ref[q, at, :] = jnp.where(done_ref[at, :] > 0, mixed, 0.0).astype(jnp.bfloat16)
            return 0

        lax.fori_loop(0, rows // row_block, block, 0)

    send_own(0)

    @pl.when(chunks > 1)
    def _():
        send_own(1)

    own_copy.wait()
    hid_copy.wait()

    def turn(t, _):
        @pl.when(t + 2 < chunks)
        def _():
            send_own(t + 2)

        @pl.when(t < chunks)
        def _():
            forward(t)

        for j in range(planes):
            last = planes + (j // 2) * group_size + 1

            @pl.when((t - 1 - j >= 1) & (t - 1 - j < n) & (t <= last))
            def _(j=j):
                kv_hop(j, t - 1 - j)

            @pl.when(t == last)
            def _(j=j):
                def rest(d, _):
                    kv_hop(j, d)
                    return 0

                lax.fori_loop(last - j, n, rest, 0)

        c = t - 1

        @pl.when(t >= 1)
        def _():
            project(c)

        @pl.when((t >= 1) & (c < planes))
        def _():
            fresh = jnp.where(lax.rem(c, 2) == 0, rotated(), acc[...]).astype(jnp.bfloat16)
            fresh = jnp.where(done_ref[...] > 0, fresh, stored[c])
            cache_ref[c] = fresh
            kvbuf[c, pl.ds(pl.multiple_of(s * rows, rows), rows), :] = fresh

            @pl.when(has_up)
            def _():
                kv_up_copy(c, s).start()

            @pl.when(has_down)
            def _():
                kv_down_copy(c, s).start()

        @pl.when(c >= planes)
        def _():
            qbuf[...] = rotated().astype(jnp.bfloat16)
            attend(c - planes)

        return 0

    lax.fori_loop(0, chunks + 1, turn, 0)

    def drain(c, _):
        def each(o, _):
            @pl.when(has_up & (o <= s))
            def _():
                up_copy(c, o, piece(c, o, g)).wait_send()

            @pl.when(has_down & (o >= s))
            def _():
                down_copy(c, o, piece(c, o, g)).wait_send()

            @pl.when(o != s)
            def _():
                for k in range(1, groups):
                    side_copy(c, o, g, lax.rem(g + k, groups)).wait_send()

            return 0

        lax.fori_loop(0, n, each, 0)
        return 0

    lax.fori_loop(0, chunks, drain, 0)

    def kv_drain(j, _):
        def each(o, _):
            @pl.when(has_up & (o <= s))
            def _():
                kv_up_copy(j, o).wait_send()

            @pl.when(has_down & (o >= s))
            def _():
                kv_down_copy(j, o).wait_send()

            return 0

        lax.fori_loop(0, n, each, 0)
        return 0

    lax.fori_loop(0, planes, kv_drain, 0)


def local(n, groups, meet_span, span_map, hidden, w_query, w_keyval, stored_kv):
    row_count, features = hidden.shape
    span_count = span_map.shape[0]
    depth, local_heads = w_query.shape[:2]
    head_width = stored_kv.shape[2] // 2
    group_size = w_query.shape[2] // head_width
    span_len = CH
    slots_dev = row_count // span_len
    planes, heads = 2 * local_heads, local_heads * group_size
    chunks = planes + heads
    offsets = jnp.arange(span_len, dtype=jnp.int32)
    key_pos = (span_map[:, None] * span_len + offsets[None, :]).reshape(1, -1)
    seq_index = lax.axis_index("seq")
    my_spans = lax.dynamic_slice_in_dim(span_map, seq_index * slots_dev, slots_dev, 0)
    positions = (my_spans[:, None] * span_len + offsets[None, :]).reshape(-1)
    computed_slot = (my_spans < meet_span[0]) | (my_spans == span_count - 1)
    done = jnp.repeat(computed_slot, span_len).astype(jnp.int32)[:, None]
    cosine, sine = rotary_tables(positions, head_width)
    own_w = jnp.concatenate(
        [
            w_keyval.reshape(depth, planes, head_width),
            w_query.reshape(depth, heads, head_width),
        ],
        1,
    ).transpose(1, 0, 2)
    stored = stored_kv.reshape(row_count, planes, head_width).transpose(1, 0, 2)
    vmem = pl.BlockSpec(memory_space=pltpu.VMEM)
    hbm = pl.BlockSpec(memory_space=pl.ANY)
    dma = pltpu.SemaphoreType.DMA
    attended, cache = pl.pallas_call(
        functools.partial(kernel, n, groups, local_heads, group_size),
        out_shape=(
            jax.ShapeDtypeStruct((heads, row_count, head_width), jnp.bfloat16),
            jax.ShapeDtypeStruct((planes, row_count, head_width), jnp.bfloat16),
        ),
        in_specs=[hbm, hbm, vmem, vmem, vmem, vmem, vmem, vmem],
        out_specs=(vmem, vmem),
        scratch_shapes=[
            pltpu.VMEM((row_count, features), jnp.bfloat16),
            pltpu.VMEM((chunks, features, head_width), jnp.bfloat16),
            pltpu.VMEM((planes, n * row_count, head_width), jnp.bfloat16),
            pltpu.VMEM((row_count, head_width), jnp.bfloat16),
            pltpu.VMEM((row_count, head_width), jnp.float32),
            dma,
            dma,
            dma((chunks, n)),
            dma((chunks, n)),
            dma((chunks, n)),
            dma((chunks, n, groups)),
            dma((chunks, n, groups)),
            dma((planes, n)),
            dma((planes, n)),
            dma((planes, n)),
        ],
        compiler_params=pltpu.CompilerParams(
            collective_id=0, has_side_effects=True, vmem_limit_bytes=58 * 1024 * 1024
        ),
    )(hidden, own_w, stored, cosine, sine, positions[:, None], done, key_pos)
    attended = attended.transpose(1, 0, 2).reshape(row_count, local_heads, -1)
    cache = cache.transpose(1, 0, 2).reshape(row_count, local_heads, -1)
    return (attended, cache)


def solution(mesh):
    return jax.shard_map(
        functools.partial(local, mesh.shape["seq"], mesh.shape["grp"]),
        mesh=mesh,
        in_specs=(
            P("grp"),
            P("grp"),
            P(("grp", "seq"), None),
            P("seq", ("head", "hold"), None),
            P("seq", ("head", "hold"), None),
            P(("grp", "seq"), ("head", "hold"), None),
        ),
        out_specs=(
            P(("grp", "seq"), ("head", "hold"), None),
            P(("grp", "seq"), ("head", "hold"), None),
        ),
        check_vma=False,
    )
```

```python
import functools
import math

import jax
import jax.numpy as jnp
from jax import lax
from jax.experimental import pallas as pl
from jax.experimental.pallas import tpu as pltpu
from jax.sharding import PartitionSpec as P

CH = 256
MESH = pl.DeviceIdType.MESH

theta_base = 500000.0
lowest = -1e30


def rotary_tables(positions, head_width):
    half_width = head_width // 2
    frequency = theta_base ** (
        -(jnp.arange(half_width, dtype=jnp.float32) * 2.0) / head_width
    )
    angles = positions.astype(jnp.float32)[:, None] * frequency[None, :]
    cosine, sine = jnp.cos(angles), jnp.sin(angles)
    return jnp.concatenate([cosine, cosine], -1), jnp.concatenate([-sine, sine], -1)


def kernel(
    n, groups, head_dev, hold_dev, local_heads, group_size,
    hidden_hbm, own_kv, own_q, stored_hbm, cos_ref, sin_ref, qpos_ref, done_ref, kpos_ref,
    out_ref, cache_ref,
    hid, wbuf, kvbuf, stored, gout, qbuf, acc,
    hid_sem, st_sem, own_sem, up_send, down_send, z_recv, y_send, y_recv,
    kv_up, kv_down, kv_recv,
    lend_send, lend_recv, x_send, x_recv, mate_send, mate_recv,
    st_send, st_recv, back_send, back_recv, ret_send, ret_recv,
):
    s = lax.axis_index("seq")
    g = lax.axis_index("grp")
    hx = lax.axis_index("head")
    hc = lax.axis_index("hold")
    planes, rows, width = cache_ref.shape
    heads = out_ref.shape[0]
    chunks = planes + heads
    depth = own_kv.shape[0]
    part = depth if groups == 1 else (depth // 16) * 9
    rest_part = depth - part
    subs = lend_send.shape[0]
    sub_width = hid.shape[1] // subs
    lent_rows = rows // (head_dev * hold_dev)
    idle = (s == 0) | (s == n - 1)
    host = (s == 1) | (s == n - 2)
    partner = jnp.where(s == 0, 1, n - 2)
    guest = jnp.where(s == 1, 0, n - 1)
    has_up, has_down = (s < n - 2) & ~idle, (s > 1) & ~idle
    near_up, near_down = s + 1 < n, s > 0
    row_groups = jnp.where(idle, 0, jnp.where(host, 2, 1))

    barrier = pltpu.get_barrier_semaphore()

    def greet(device):
        pl.semaphore_signal(barrier, inc=1, device_id=device, device_id_type=MESH)

    @pl.when(near_up)
    def _():
        greet({"seq": s + 1})

    @pl.when(near_down)
    def _():
        greet({"seq": s - 1})

    for k in range(1, groups):
        greet({"grp": lax.rem(g + k, groups)})
    for k in range(1, head_dev):
        greet({"head": lax.rem(hx + k, head_dev)})
    for k in range(1, hold_dev):
        greet({"hold": lax.rem(hc + k, hold_dev)})

    def columns(c):
        return pl.ds(pl.multiple_of(c * width, width), width)

    def row_range(i):
        return pl.ds(pl.multiple_of(i * rows, rows), rows)

    hid_copy = pltpu.make_async_copy(hidden_hbm, hid.at[pl.ds(0, rows), :], hid_sem)
    hid_copy.start()
    st_copy = pltpu.make_async_copy(stored_hbm, stored.at[:, pl.ds(0, rows), :], st_sem)
    st_copy.start()

    def own_copy(c):
        own = own_kv.at[:, columns(c)] if c < planes else own_q.at[:, columns(c - planes)]
        return pltpu.make_async_copy(
            own, wbuf.at[c, pl.ds(pl.multiple_of(s * depth, depth), depth), :], own_sem.at[c]
        )

    for c in range(chunks):
        own_copy(c).start()
    pl.semaphore_wait(
        barrier,
        jnp.where(near_up, 1, 0) + jnp.where(near_down, 1, 0)
        + (groups - 1 + head_dev - 1 + hold_dev - 1),
    )

    def piece(c, o):
        return wbuf.at[c, pl.ds(pl.multiple_of(o * depth + g * rest_part, 16), part), :]

    def side_piece(c, o, sender):
        return wbuf.at[c, pl.ds(pl.multiple_of(o * depth + sender * part, 16), rest_part), :]

    def kv_piece(j, o):
        return kvbuf.at[j, row_range(o), :]

    def remote(src, dst, send_sem, recv_sem, **device):
        return pltpu.make_async_remote_copy(
            src_ref=src, dst_ref=dst, send_sem=send_sem, recv_sem=recv_sem,
            device_id=device, device_id_type=MESH,
        )

    def up_copy(c, o, src=None):
        src = piece(c, o) if src is None else src
        return remote(src, piece(c, o), up_send.at[c, o], z_recv.at[c, o], seq=s + 1)

    def down_copy(c, o, src=None):
        src = piece(c, o) if src is None else src
        return remote(src, piece(c, o), down_send.at[c, o], z_recv.at[c, o], seq=s - 1)

    def side_copy(c, o, sender, target):
        at = side_piece(c, o, sender)
        return remote(at, at, y_send.at[c, o], y_recv.at[c, o], grp=target)

    def kv_up_copy(j, o):
        at = kv_piece(j, o)
        return remote(at, at, kv_up.at[j, o], kv_recv.at[j, o], seq=s + 1)

    def kv_down_copy(j, o):
        at = kv_piece(j, o)
        return remote(at, at, kv_down.at[j, o], kv_recv.at[j, o], seq=s - 1)

    def hid_piece(x, h, k):
        start = rows + (x * hold_dev + h) * lent_rows
        return hid.at[
            pl.ds(pl.multiple_of(start, 16), lent_rows), pl.ds(k * sub_width, sub_width)
        ]

    def lend_copy(k):
        start = (hx * hold_dev + hc) * lent_rows
        src = hidden_hbm.at[
            pl.ds(pl.multiple_of(start, 16), lent_rows), pl.ds(k * sub_width, sub_width)
        ]
        return remote(src, hid_piece(hx, hc, k), lend_send.at[k], lend_recv.at[k], seq=partner)

    def x_copy(k, x, target):
        at = hid_piece(x, hc, k)
        return remote(at, at, x_send.at[k, target], x_recv.at[k, x], head=target)

    def mate_copy(k, x, h, target):
        at = hid_piece(x, h, k)
        return remote(at, at, mate_send.at[k, x, target], mate_recv.at[k, x, h], hold=target)

    def st_lend():
        return remote(
            stored_hbm, stored.at[:, pl.ds(rows, rows), :], st_send, st_recv, seq=partner
        )

    def back_copy(j):
        return remote(
            kv_piece(j, guest), cache_ref.at[j], back_send.at[j], back_recv.at[j], seq=guest
        )

    def ret_copy(q):
        return remote(gout.at[q], out_ref.at[q], ret_send.at[q], ret_recv.at[q], seq=guest)

    def send_own(c):
        at = pl.ds(pl.multiple_of(g * rest_part, 16), part)
        src = own_kv.at[at, columns(c)] if c < planes else own_q.at[at, columns(c - planes)]

        @pl.when(has_up)
        def _():
            up_copy(c, s, src).start()

        @pl.when(has_down)
        def _():
            down_copy(c, s, src).start()

    def spread(c, o):
        for k in range(1, groups):
            side_copy(c, o, g, lax.rem(g + k, groups)).start()

    def forward(c):
        def hop(d, _):
            lo, hi = s - d, s + d

            @pl.when((lo >= 0) & ~idle)
            def _():
                up_copy(c, lo).wait_recv()

                @pl.when(has_up)
                def _():
                    up_copy(c, lo).start()

                spread(c, lo)

            @pl.when((hi < n) & ~idle)
            def _():
                down_copy(c, hi).wait_recv()

                @pl.when(has_down)
                def _():
                    down_copy(c, hi).start()

                spread(c, hi)

            return 0

        lax.fori_loop(1, n, hop, 0)

    def kv_hop(j, d):
        lo, hi = s - d, s + d

        @pl.when((lo >= 0) & (s > 1) & ~idle)
        def _():
            kv_up_copy(j, lo).wait_recv()

            @pl.when(has_up)
            def _():
                kv_up_copy(j, lo).start()

        @pl.when((hi < n) & (s < n - 2) & ~idle)
        def _():
            kv_down_copy(j, hi).wait_recv()

            @pl.when(has_down)
            def _():
                kv_down_copy(j, hi).start()

    def gather_side(c):
        def each(o, _):
            @pl.when((o != s) & ~idle)
            def _():
                for k in range(1, groups):
                    side_copy(c, o, lax.rem(g + k, groups), g).wait_recv()

            return 0

        lax.fori_loop(0, n, each, 0)

    def project(c, r):
        acc[...] = jnp.zeros_like(acc)

        def add(o, _):
            at = pl.ds(pl.multiple_of(o * depth, depth), depth)
            acc[...] += jnp.dot(
                hid[row_range(r), at], wbuf[c, at, :], preferred_element_type=jnp.float32
            )
            return 0

        lax.fori_loop(0, n, add, 0)

    def rotated(r):
        raw = acc[...]
        half = width // 2
        turned = jnp.concatenate([raw[:, half:], raw[:, :half]], -1)
        return raw * cos_ref[row_range(r), :] + turned * sin_ref[row_range(r), :]

    def make_plane(c, r):
        project(c, r)
        fresh = jnp.where(lax.rem(c, 2) == 0, rotated(r), acc[...]).astype(jnp.bfloat16)
        fresh = jnp.where(done_ref[row_range(r), :] > 0, fresh, stored[c, row_range(r), :])
        o = jnp.where(r == 0, s, guest)
        kvbuf[c, row_range(o), :] = fresh

        @pl.when(r == 0)
        def _():
            cache_ref[c] = fresh

        @pl.when(r == 1)
        def _():
            back_copy(c).start()

        @pl.when(has_up)
        def _():
            kv_up_copy(c, o).start()

        @pl.when(has_down)
        def _():
            kv_down_copy(c, o).start()

    row_block = 128
    scale = width ** (-0.5) * math.log2(math.e)

    def attend(q, r):
        head = q // group_size

        def block(b, _):
            at = pl.ds(pl.multiple_of(b * row_block, row_block), row_block)
            full = pl.ds(pl.multiple_of(r * rows + b * row_block, row_block), row_block)
            scores = lax.dot_general(
                qbuf[at, :], kvbuf[2 * head], (((1,), (1,)), ((), ())),
                preferred_element_type=jnp.float32,
            ) * scale
            scores = jnp.where(kpos_ref[...] <= qpos_ref[full, :], scores, lowest)
            top = scores.max(-1, keepdims=True)
            weights = jnp.exp2(scores - top)
            total = weights.sum(-1, keepdims=True)
            mixed = jnp.dot(
                weights.astype(jnp.bfloat16), kvbuf[2 * head + 1],
                preferred_element_type=jnp.float32,
            ) / total
            mixed = jnp.where(done_ref[full, :] > 0, mixed, 0.0).astype(jnp.bfloat16)

            @pl.when(r == 0)
            def _():
                out_ref[q, at, :] = mixed

            @pl.when(r == 1)
            def _():
                gout[q, at, :] = mixed

            return 0

        lax.fori_loop(0, rows // row_block, block, 0)

        @pl.when(r == 1)
        def _():
            ret_copy(q).start()

    for c in range(planes):
        send_own(c)

    @pl.when(idle)
    def _():
        def own_to_partner(c):
            at = pl.ds(pl.multiple_of(g * rest_part, 16), part)
            src = own_kv.at[at, columns(c)] if c < planes else own_q.at[at, columns(c - planes)]

            @pl.when(s == 0)
            def _():
                up_copy(c, s, src).start()

            @pl.when(s == n - 1)
            def _():
                down_copy(c, s, src).start()

        for c in range(chunks):
            if c == planes:
                for k in range(subs):
                    lend_copy(k).start()
                st_lend().start()
            own_to_partner(c)

    for c in range(chunks):
        own_copy(c).wait()
    hid_copy.wait()
    st_copy.wait()

    def early(t, _):
        @pl.when(t < planes)
        def _():
            forward(t)

        @pl.when(t == planes - 1)
        def _():
            for c in range(planes, chunks):
                send_own(c)

        @pl.when(t >= 1)
        def _():
            gather_side(t - 1)

            @pl.when(~idle)
            def _():
                make_plane(t - 1, 0)

        return 0

    lax.fori_loop(0, planes + 1, early, 0)

    @pl.when(host)
    def _():
        for k in range(subs):
            lend_copy_in = remote(
                hid_piece(hx, hc, k), hid_piece(hx, hc, k),
                lend_send.at[k], lend_recv.at[k], seq=guest,
            )
            lend_copy_in.wait_recv()
            for i in range(1, head_dev):
                x_copy(k, hx, lax.rem(hx + i, head_dev)).start()
            for i in range(1, hold_dev):
                mate_copy(k, hx, hc, lax.rem(hc + i, hold_dev)).start()
        for k in range(subs):
            for i in range(1, head_dev):
                x = lax.rem(hx + i, head_dev)
                x_copy(k, x, hx).wait_recv()
                for m in range(1, hold_dev):
                    mate_copy(k, x, hc, lax.rem(hc + m, hold_dev)).start()
        for k in range(subs):
            for x in range(head_dev):
                for m in range(1, hold_dev):
                    mate_copy(k, x, lax.rem(hc + m, hold_dev), hc).wait_recv()
        st_in = stored.at[:, pl.ds(rows, rows), :]
        remote(st_in, st_in, st_send, st_recv, seq=guest).wait_recv()

        def guest_plane(c, _):
            make_plane(c, 1)
            return 0

        lax.fori_loop(0, planes, guest_plane, 0)

    def late(t, _):
        @pl.when(t < chunks)
        def _():
            forward(t)

        c = t - 1

        @pl.when(c >= planes)
        def _():
            gather_side(c)
            q = c - planes

            @pl.when(lax.rem(q, group_size) == 0)
            def _():
                def rest(d, _):
                    kv_hop(2 * (q // group_size), d)
                    kv_hop(2 * (q // group_size) + 1, d)
                    return 0

                lax.fori_loop(1, n, rest, 0)

            def each(r, _):
                project(c, r)
                qbuf[...] = rotated(r).astype(jnp.bfloat16)
                attend(q, r)
                return 0

            lax.fori_loop(0, row_groups, each, 0)

        return 0

    lax.fori_loop(planes, chunks + 1, late, 0)

    def drain(c, _):
        def each(o, _):
            @pl.when((has_up & (o <= s)) | ((s == 0) & (o == 0)))
            def _():
                up_copy(c, o).wait_send()

            @pl.when((has_down & (o >= s)) | ((s == n - 1) & (o == n - 1)))
            def _():
                down_copy(c, o).wait_send()

            @pl.when((o != s) & ~idle)
            def _():
                for k in range(1, groups):
                    side_copy(c, o, g, lax.rem(g + k, groups)).wait_send()

            return 0

        lax.fori_loop(0, n, each, 0)
        return 0

    lax.fori_loop(0, chunks, drain, 0)

    def kv_drain(j, _):
        def each(o, _):
            @pl.when(has_up & (o <= s))
            def _():
                kv_up_copy(j, o).wait_send()

            @pl.when(has_down & (o >= s))
            def _():
                kv_down_copy(j, o).wait_send()

            return 0

        lax.fori_loop(0, n, each, 0)

        @pl.when(host)
        def _():
            back_copy(j).wait_send()

        @pl.when(idle)
        def _():
            at = cache_ref.at[j]
            remote(at, at, back_send.at[j], back_recv.at[j], seq=partner).wait_recv()

        return 0

    lax.fori_loop(0, planes, kv_drain, 0)

    @pl.when(host)
    def _():
        for k in range(subs):
            for i in range(1, head_dev):
                x_copy(k, hx, lax.rem(hx + i, head_dev)).wait_send()
            for x in range(head_dev):
                for m in range(1, hold_dev):
                    mate_copy(k, x, hc, lax.rem(hc + m, hold_dev)).wait_send()
        for q in range(heads):
            ret_copy(q).wait_send()

    @pl.when(idle)
    def _():
        for k in range(subs):
            lend_copy(k).wait_send()
        st_lend().wait_send()
        for q in range(heads):
            at = out_ref.at[q]
            remote(at, at, ret_send.at[q], ret_recv.at[q], seq=partner).wait_recv()


def local(n, groups, head_dev, hold_dev, meet_span, span_map, hidden, w_query, w_keyval, stored_kv):
    row_count, features = hidden.shape
    span_count = span_map.shape[0]
    depth, local_heads = w_query.shape[:2]
    head_width = stored_kv.shape[2] // 2
    group_size = w_query.shape[2] // head_width
    span_len = CH
    slots_dev = row_count // span_len
    planes, heads = 2 * local_heads, local_heads * group_size
    chunks = planes + heads
    offsets = jnp.arange(span_len, dtype=jnp.int32)
    key_pos = (span_map[:, None] * span_len + offsets[None, :]).reshape(1, -1)
    seq_index = lax.axis_index("seq")
    guest = jnp.where(seq_index == 1, 0, n - 1)
    my_spans = jnp.concatenate(
        [
            lax.dynamic_slice_in_dim(span_map, index * slots_dev, slots_dev, 0)
            for index in (seq_index, guest)
        ]
    )
    positions = (my_spans[:, None] * span_len + offsets[None, :]).reshape(-1)
    computed_slot = (my_spans < meet_span[0]) | (my_spans == span_count - 1)
    done = jnp.repeat(computed_slot, span_len).astype(jnp.int32)[:, None]
    cosine, sine = rotary_tables(positions, head_width)
    own_kv = w_keyval.reshape(depth, planes * head_width)
    own_q = w_query.reshape(depth, heads * head_width)
    stored = stored_kv.reshape(row_count, planes, head_width).transpose(1, 0, 2)
    subs = 4
    vmem = pl.BlockSpec(memory_space=pltpu.VMEM)
    hbm = pl.BlockSpec(memory_space=pl.ANY)
    dma = pltpu.SemaphoreType.DMA
    attended, cache = pl.pallas_call(
        functools.partial(kernel, n, groups, head_dev, hold_dev, local_heads, group_size),
        out_shape=(
            jax.ShapeDtypeStruct((heads, row_count, head_width), jnp.bfloat16),
            jax.ShapeDtypeStruct((planes, row_count, head_width), jnp.bfloat16),
        ),
        in_specs=[hbm] * 4 + [vmem] * 5,
        out_specs=(vmem, vmem),
        scratch_shapes=[
            pltpu.VMEM((2 * row_count, features), jnp.bfloat16),
            pltpu.VMEM((chunks, features, head_width), jnp.bfloat16),
            pltpu.VMEM((planes, n * row_count, head_width), jnp.bfloat16),
            pltpu.VMEM((planes, 2 * row_count, head_width), jnp.bfloat16),
            pltpu.VMEM((heads, row_count, head_width), jnp.bfloat16),
            pltpu.VMEM((row_count, head_width), jnp.bfloat16),
            pltpu.VMEM((row_count, head_width), jnp.float32),
            dma,
            dma,
            dma((chunks,)),
        ]
        + [dma((chunks, n))] * 5
        + [dma((planes, n))] * 3
        + [dma((subs,))] * 2
        + [dma((subs, head_dev))] * 2
        + [dma((subs, head_dev, hold_dev))] * 2
        + [dma] * 2
        + [dma((planes,))] * 2
        + [dma((heads,))] * 2,
        compiler_params=pltpu.CompilerParams(
            collective_id=0, has_side_effects=True, vmem_limit_bytes=60 * 1024 * 1024
        ),
    )(hidden, own_kv, own_q, stored, cosine, sine, positions[:, None], done, key_pos)
    attended = attended.transpose(1, 0, 2).reshape(row_count, local_heads, -1)
    cache = cache.transpose(1, 0, 2).reshape(row_count, local_heads, -1)
    return (attended, cache)


def solution(mesh):
    return jax.shard_map(
        functools.partial(local, *(mesh.shape[a] for a in ("seq", "grp", "head", "hold"))),
        mesh=mesh,
        in_specs=(
            P("grp"),
            P("grp"),
            P(("grp", "seq"), None),
            P("seq", ("head", "hold"), None),
            P("seq", ("head", "hold"), None),
            P(("grp", "seq"), ("head", "hold"), None),
        ),
        out_specs=(
            P(("grp", "seq"), ("head", "hold"), None),
            P(("grp", "seq"), ("head", "hold"), None),
        ),
        check_vma=False,
    )
```

```python
import functools
import math

import jax
import jax.numpy as jnp
from jax import lax
from jax.experimental import pallas as pl
from jax.experimental.pallas import tpu as pltpu
from jax.sharding import PartitionSpec as P

CH = 256
MESH = pl.DeviceIdType.MESH

theta_base = 500000.0
lowest = -1e30


def rotary_tables(positions, head_width):
    half_width = head_width // 2
    frequency = theta_base ** (
        -(jnp.arange(half_width, dtype=jnp.float32) * 2.0) / head_width
    )
    angles = positions.astype(jnp.float32)[:, None] * frequency[None, :]
    cosine, sine = jnp.cos(angles), jnp.sin(angles)
    return jnp.concatenate([cosine, cosine], -1), jnp.concatenate([-sine, sine], -1)


def kernel(
    n, groups, head_dev, hold_dev, local_heads, group_size,
    hidden_hbm, own_kv, own_q, stored_hbm, cos_ref, sin_ref, qpos_ref, done_ref, done_row, kpos_ref,
    out_ref, cache_ref,
    hid, wbuf, kvbuf, stored, gout, turned_values, acc,
    hid_sem, st_sem, own_sem, up_send, down_send, z_recv, y_send, y_recv,
    kv_up, kv_down, kv_recv,
    lend_send, lend_recv, x_send, x_recv, mate_send, mate_recv,
    st_send, st_recv, back_send, back_recv, ret_send, ret_recv,
):
    s = lax.axis_index("seq")
    g = lax.axis_index("grp")
    hx = lax.axis_index("head")
    hc = lax.axis_index("hold")
    planes, rows, width = cache_ref.shape
    heads = out_ref.shape[0]
    chunks = planes + heads
    depth = own_kv.shape[0]
    part = depth if groups == 1 else (depth // 16) * 9
    rest_part = depth - part
    subs = lend_send.shape[0]
    sub_width = hid.shape[1] // subs
    lent_rows = rows // (head_dev * hold_dev)
    idle = (s == 0) | (s == n - 1)
    host = (s == 1) | (s == n - 2)
    partner = jnp.where(s == 0, 1, n - 2)
    guest = jnp.where(s == 1, 0, n - 1)
    has_up, has_down = (s < n - 2) & ~idle, (s > 1) & ~idle
    near_up, near_down = s + 1 < n, s > 0
    row_groups = jnp.where(idle, 0, jnp.where(host, 2, 1))

    barrier = pltpu.get_barrier_semaphore()

    def greet(device):
        pl.semaphore_signal(barrier, inc=1, device_id=device, device_id_type=MESH)

    @pl.when(near_up)
    def _():
        greet({"seq": s + 1})

    @pl.when(near_down)
    def _():
        greet({"seq": s - 1})

    for k in range(1, groups):
        greet({"grp": lax.rem(g + k, groups)})
    for k in range(1, head_dev):
        greet({"head": lax.rem(hx + k, head_dev)})
    for k in range(1, hold_dev):
        greet({"hold": lax.rem(hc + k, hold_dev)})

    def columns(c):
        return pl.ds(pl.multiple_of(c * width, width), width)

    def row_range(i):
        return pl.ds(pl.multiple_of(i * rows, rows), rows)

    hid_copy = pltpu.make_async_copy(hidden_hbm, hid.at[pl.ds(0, rows), :], hid_sem)
    hid_copy.start()
    st_copy = pltpu.make_async_copy(stored_hbm, stored.at[:, pl.ds(0, rows), :], st_sem)
    st_copy.start()

    def own_copy(c):
        own = own_kv.at[:, columns(c)] if c < planes else own_q.at[:, columns(c - planes)]
        return pltpu.make_async_copy(
            own, wbuf.at[c, pl.ds(pl.multiple_of(s * depth, depth), depth), :], own_sem.at[c]
        )

    for c in range(chunks):
        own_copy(c).start()
    pl.semaphore_wait(
        barrier,
        jnp.where(near_up, 1, 0) + jnp.where(near_down, 1, 0)
        + (groups - 1 + head_dev - 1 + hold_dev - 1),
    )

    def piece(c, o):
        return wbuf.at[c, pl.ds(pl.multiple_of(o * depth + g * rest_part, 16), part), :]

    def side_piece(c, o, sender):
        return wbuf.at[c, pl.ds(pl.multiple_of(o * depth + sender * part, 16), rest_part), :]

    def kv_piece(j, o):
        return kvbuf.at[j, row_range(o), :]

    def remote(src, dst, send_sem, recv_sem, **device):
        return pltpu.make_async_remote_copy(
            src_ref=src, dst_ref=dst, send_sem=send_sem, recv_sem=recv_sem,
            device_id=device, device_id_type=MESH,
        )

    def up_copy(c, o, src=None):
        src = piece(c, o) if src is None else src
        return remote(src, piece(c, o), up_send.at[c, o], z_recv.at[c, o], seq=s + 1)

    def down_copy(c, o, src=None):
        src = piece(c, o) if src is None else src
        return remote(src, piece(c, o), down_send.at[c, o], z_recv.at[c, o], seq=s - 1)

    def side_copy(c, o, sender, target):
        at = side_piece(c, o, sender)
        return remote(at, at, y_send.at[c, o], y_recv.at[c, o], grp=target)

    def kv_up_copy(j, o):
        at = kv_piece(j, o)
        return remote(at, at, kv_up.at[j, o], kv_recv.at[j, o], seq=s + 1)

    def kv_down_copy(j, o):
        at = kv_piece(j, o)
        return remote(at, at, kv_down.at[j, o], kv_recv.at[j, o], seq=s - 1)

    def hid_piece(x, h, k):
        start = rows + (x * hold_dev + h) * lent_rows
        return hid.at[
            pl.ds(pl.multiple_of(start, 16), lent_rows), pl.ds(k * sub_width, sub_width)
        ]

    def lend_copy(k):
        start = (hx * hold_dev + hc) * lent_rows
        src = hidden_hbm.at[
            pl.ds(pl.multiple_of(start, 16), lent_rows), pl.ds(k * sub_width, sub_width)
        ]
        return remote(src, hid_piece(hx, hc, k), lend_send.at[k], lend_recv.at[k], seq=partner)

    def x_copy(k, x, target):
        at = hid_piece(x, hc, k)
        return remote(at, at, x_send.at[k, target], x_recv.at[k, x], head=target)

    def mate_copy(k, x, h, target):
        at = hid_piece(x, h, k)
        return remote(at, at, mate_send.at[k, x, target], mate_recv.at[k, x, h], hold=target)

    def st_lend():
        return remote(
            stored_hbm, stored.at[:, pl.ds(rows, rows), :], st_send, st_recv, seq=partner
        )

    def back_copy(j):
        return remote(
            kv_piece(j, guest), cache_ref.at[j], back_send.at[j], back_recv.at[j], seq=guest
        )

    def ret_copy(q):
        return remote(gout.at[q], out_ref.at[q], ret_send.at[q], ret_recv.at[q], seq=guest)

    def send_own(c):
        at = pl.ds(pl.multiple_of(g * rest_part, 16), part)
        src = own_kv.at[at, columns(c)] if c < planes else own_q.at[at, columns(c - planes)]

        @pl.when(has_up)
        def _():
            up_copy(c, s, src).start()

        @pl.when(has_down)
        def _():
            down_copy(c, s, src).start()

    def spread(c, o):
        for k in range(1, groups):
            side_copy(c, o, g, lax.rem(g + k, groups)).start()

    def forward(c):
        def hop(d, _):
            lo, hi = s - d, s + d

            @pl.when((lo >= 0) & ~idle)
            def _():
                up_copy(c, lo).wait_recv()

                @pl.when(has_up)
                def _():
                    up_copy(c, lo).start()

                spread(c, lo)

            @pl.when((hi < n) & ~idle)
            def _():
                down_copy(c, hi).wait_recv()

                @pl.when(has_down)
                def _():
                    down_copy(c, hi).start()

                spread(c, hi)

            return 0

        lax.fori_loop(1, n, hop, 0)

    def kv_hop(j, d):
        lo, hi = s - d, s + d

        @pl.when((lo >= 0) & (s > 1) & ~idle)
        def _():
            kv_up_copy(j, lo).wait_recv()

            @pl.when(has_up)
            def _():
                kv_up_copy(j, lo).start()

        @pl.when((hi < n) & (s < n - 2) & ~idle)
        def _():
            kv_down_copy(j, hi).wait_recv()

            @pl.when(has_down)
            def _():
                kv_down_copy(j, hi).start()

    def gather_side(c):
        def each(o, _):
            @pl.when((o != s) & ~idle)
            def _():
                for k in range(1, groups):
                    side_copy(c, o, lax.rem(g + k, groups), g).wait_recv()

            return 0

        lax.fori_loop(0, n, each, 0)

    def project(c, r):
        acc[...] = jnp.zeros_like(acc)

        def add(o, _):
            at = pl.ds(pl.multiple_of(o * depth, depth), depth)
            pair = jnp.concatenate([wbuf[c, at, :], wbuf[c + 1, at, :]], -1)
            acc[...] += jnp.dot(
                hid[row_range(r), at], pair, preferred_element_type=jnp.float32
            )
            return 0

        lax.fori_loop(0, n, add, 0)

    def rotated(raw, r):
        half = width // 2
        turned = jnp.concatenate([raw[:, half:], raw[:, :half]], -1)
        return raw * cos_ref[row_range(r), :] + turned * sin_ref[row_range(r), :]

    def make_planes(h, r):
        project(2 * h, r)
        o = jnp.where(r == 0, s, guest)
        for i in range(2):
            c = 2 * h + i
            raw = acc[:, i * width:(i + 1) * width]
            fresh = (rotated(raw, r) if i == 0 else raw).astype(jnp.bfloat16)
            fresh = jnp.where(done_ref[row_range(r), :] > 0, fresh, stored[c, row_range(r), :])
            kvbuf[c, row_range(o), :] = fresh

            @pl.when(r == 0)
            def _():
                cache_ref[c] = fresh

            @pl.when(r == 1)
            def _():
                back_copy(c).start()

            @pl.when(has_up)
            def _():
                kv_up_copy(c, o).start()

            @pl.when(has_down)
            def _():
                kv_down_copy(c, o).start()

    row_block = 256
    scale = width ** (-0.5) * math.log2(math.e)

    def attend(q, r, i):
        head = q // group_size

        def block(b, _):
            at = pl.ds(pl.multiple_of(b * row_block, row_block), row_block)
            full = pl.ds(pl.multiple_of(r * rows + b * row_block, row_block), row_block)
            raw = acc[at, i * width:(i + 1) * width]
            half = width // 2
            turned = jnp.concatenate([raw[:, half:], raw[:, :half]], -1)
            queries = (raw * cos_ref[full, :] + turned * sin_ref[full, :]).astype(jnp.bfloat16)
            scores = lax.dot_general(
                kvbuf[2 * head], queries, (((1,), (1,)), ((), ())),
                preferred_element_type=jnp.float32,
            ) * scale
            key_pos = jnp.concatenate([kpos_ref[...]] * (row_block // width), -1)
            scores = jnp.where(key_pos <= qpos_ref[:, full], scores, lowest)
            top = scores.max(0, keepdims=True)
            weights = jnp.exp2(scores - top)
            total = weights.sum(0, keepdims=True)
            mixed = jnp.dot(
                turned_values[...], weights.astype(jnp.bfloat16),
                preferred_element_type=jnp.float32,
            ) / total
            mixed = jnp.where(done_row[:, full] > 0, mixed, 0.0).T.astype(jnp.bfloat16)

            @pl.when(r == 0)
            def _():
                out_ref[q, at, :] = mixed

            @pl.when(r == 1)
            def _():
                gout[q, at, :] = mixed

            return 0

        lax.fori_loop(0, rows // row_block, block, 0)

        @pl.when(r == 1)
        def _():
            ret_copy(q).start()

    for c in range(planes):
        send_own(c)

    @pl.when(idle)
    def _():
        def own_to_partner(c):
            at = pl.ds(pl.multiple_of(g * rest_part, 16), part)
            src = own_kv.at[at, columns(c)] if c < planes else own_q.at[at, columns(c - planes)]

            @pl.when(s == 0)
            def _():
                up_copy(c, s, src).start()

            @pl.when(s == n - 1)
            def _():
                down_copy(c, s, src).start()

        for c in range(chunks):
            if c == planes:
                for k in range(subs):
                    lend_copy(k).start()
                st_lend().start()
            own_to_partner(c)

    for c in range(chunks):
        own_copy(c).wait()
    hid_copy.wait()
    st_copy.wait()

    def early(t, _):
        @pl.when(t < local_heads)
        def _():
            forward(2 * t)
            forward(2 * t + 1)

        @pl.when(t == local_heads - 1)
        def _():
            for c in range(planes, chunks):
                send_own(c)

        @pl.when(t >= 1)
        def _():
            gather_side(2 * t - 2)
            gather_side(2 * t - 1)

            @pl.when(~idle)
            def _():
                make_planes(t - 1, 0)

        return 0

    lax.fori_loop(0, local_heads + 1, early, 0)

    @pl.when(host)
    def _():
        for k in range(subs):
            lend_copy_in = remote(
                hid_piece(hx, hc, k), hid_piece(hx, hc, k),
                lend_send.at[k], lend_recv.at[k], seq=guest,
            )
            lend_copy_in.wait_recv()
            for i in range(1, head_dev):
                x_copy(k, hx, lax.rem(hx + i, head_dev)).start()
            for i in range(1, hold_dev):
                mate_copy(k, hx, hc, lax.rem(hc + i, hold_dev)).start()
        for k in range(subs):
            for i in range(1, head_dev):
                x = lax.rem(hx + i, head_dev)
                x_copy(k, x, hx).wait_recv()
                for m in range(1, hold_dev):
                    mate_copy(k, x, hc, lax.rem(hc + m, hold_dev)).start()
        for k in range(subs):
            for x in range(head_dev):
                for m in range(1, hold_dev):
                    mate_copy(k, x, lax.rem(hc + m, hold_dev), hc).wait_recv()
        st_in = stored.at[:, pl.ds(rows, rows), :]
        remote(st_in, st_in, st_send, st_recv, seq=guest).wait_recv()

        def guest_planes(h, _):
            make_planes(h, 1)
            return 0

        lax.fori_loop(0, local_heads, guest_planes, 0)

    def late(t, _):
        @pl.when(t < heads // 2)
        def _():
            forward(planes + 2 * t)
            forward(planes + 2 * t + 1)

        @pl.when(t >= 1)
        def _():
            q = 2 * (t - 1)
            c = planes + q
            gather_side(c)
            gather_side(c + 1)

            @pl.when((lax.rem(q, group_size) == 0) & ~idle)
            def _():
                head = q // group_size

                def rest(d, _):
                    kv_hop(2 * head, d)
                    kv_hop(2 * head + 1, d)
                    return 0

                lax.fori_loop(1, n, rest, 0)
                turned_values[...] = kvbuf[2 * head + 1].T

            def each(r, _):
                project(c, r)
                attend(q, r, 0)
                attend(q + 1, r, 1)
                return 0

            lax.fori_loop(0, row_groups, each, 0)

        return 0

    lax.fori_loop(0, heads // 2 + 1, late, 0)

    def drain(c, _):
        def each(o, _):
            @pl.when((has_up & (o <= s)) | ((s == 0) & (o == 0)))
            def _():
                up_copy(c, o).wait_send()

            @pl.when((has_down & (o >= s)) | ((s == n - 1) & (o == n - 1)))
            def _():
                down_copy(c, o).wait_send()

            @pl.when((o != s) & ~idle)
            def _():
                for k in range(1, groups):
                    side_copy(c, o, g, lax.rem(g + k, groups)).wait_send()

            return 0

        lax.fori_loop(0, n, each, 0)
        return 0

    lax.fori_loop(0, chunks, drain, 0)

    def kv_drain(j, _):
        def each(o, _):
            @pl.when(has_up & (o <= s))
            def _():
                kv_up_copy(j, o).wait_send()

            @pl.when(has_down & (o >= s))
            def _():
                kv_down_copy(j, o).wait_send()

            return 0

        lax.fori_loop(0, n, each, 0)

        @pl.when(host)
        def _():
            back_copy(j).wait_send()

        @pl.when(idle)
        def _():
            at = cache_ref.at[j]
            remote(at, at, back_send.at[j], back_recv.at[j], seq=partner).wait_recv()

        return 0

    lax.fori_loop(0, planes, kv_drain, 0)

    @pl.when(host)
    def _():
        for k in range(subs):
            for i in range(1, head_dev):
                x_copy(k, hx, lax.rem(hx + i, head_dev)).wait_send()
            for x in range(head_dev):
                for m in range(1, hold_dev):
                    mate_copy(k, x, hc, lax.rem(hc + m, hold_dev)).wait_send()
        for q in range(heads):
            ret_copy(q).wait_send()

    @pl.when(idle)
    def _():
        for k in range(subs):
            lend_copy(k).wait_send()
        st_lend().wait_send()
        for q in range(heads):
            at = out_ref.at[q]
            remote(at, at, ret_send.at[q], ret_recv.at[q], seq=partner).wait_recv()


def local(n, groups, head_dev, hold_dev, meet_span, span_map, hidden, w_query, w_keyval, stored_kv):
    row_count, features = hidden.shape
    span_count = span_map.shape[0]
    depth, local_heads = w_query.shape[:2]
    head_width = stored_kv.shape[2] // 2
    group_size = w_query.shape[2] // head_width
    span_len = CH
    slots_dev = row_count // span_len
    planes, heads = 2 * local_heads, local_heads * group_size
    chunks = planes + heads
    offsets = jnp.arange(span_len, dtype=jnp.int32)
    key_pos = (span_map[:, None] * span_len + offsets[None, :]).reshape(-1, 1)
    key_pos = jnp.broadcast_to(key_pos, (key_pos.shape[0], head_width))
    seq_index = lax.axis_index("seq")
    guest = jnp.where(seq_index == 1, 0, n - 1)
    my_spans = jnp.concatenate(
        [
            lax.dynamic_slice_in_dim(span_map, index * slots_dev, slots_dev, 0)
            for index in (seq_index, guest)
        ]
    )
    positions = (my_spans[:, None] * span_len + offsets[None, :]).reshape(-1)
    computed_slot = (my_spans < meet_span[0]) | (my_spans == span_count - 1)
    done = jnp.repeat(computed_slot, span_len).astype(jnp.int32)[:, None]
    cosine, sine = rotary_tables(positions, head_width)
    own_kv = w_keyval.reshape(depth, planes * head_width)
    own_q = w_query.reshape(depth, heads * head_width)
    stored = stored_kv.reshape(row_count, planes, head_width).transpose(1, 0, 2)
    subs = 4
    vmem = pl.BlockSpec(memory_space=pltpu.VMEM)
    hbm = pl.BlockSpec(memory_space=pl.ANY)
    dma = pltpu.SemaphoreType.DMA
    attended, cache = pl.pallas_call(
        functools.partial(kernel, n, groups, head_dev, hold_dev, local_heads, group_size),
        out_shape=(
            jax.ShapeDtypeStruct((heads, row_count, head_width), jnp.bfloat16),
            jax.ShapeDtypeStruct((planes, row_count, head_width), jnp.bfloat16),
        ),
        in_specs=[hbm] * 4 + [vmem] * 6,
        out_specs=(vmem, vmem),
        scratch_shapes=[
            pltpu.VMEM((2 * row_count, features), jnp.bfloat16),
            pltpu.VMEM((chunks, features, head_width), jnp.bfloat16),
            pltpu.VMEM((planes, n * row_count, head_width), jnp.bfloat16),
            pltpu.VMEM((planes, 2 * row_count, head_width), jnp.bfloat16),
            pltpu.VMEM((heads, row_count, head_width), jnp.bfloat16),
            pltpu.VMEM((head_width, n * row_count), jnp.bfloat16),
            pltpu.VMEM((row_count, 2 * head_width), jnp.float32),
            dma,
            dma,
            dma((chunks,)),
        ]
        + [dma((chunks, n))] * 5
        + [dma((planes, n))] * 3
        + [dma((subs,))] * 2
        + [dma((subs, head_dev))] * 2
        + [dma((subs, head_dev, hold_dev))] * 2
        + [dma] * 2
        + [dma((planes,))] * 2
        + [dma((heads,))] * 2,
        compiler_params=pltpu.CompilerParams(
            collective_id=0, has_side_effects=True, vmem_limit_bytes=60 * 1024 * 1024
        ),
    )(hidden, own_kv, own_q, stored, cosine, sine, positions[None, :], done, done.reshape(1, -1), key_pos)
    attended = attended.transpose(1, 0, 2).reshape(row_count, local_heads, -1)
    cache = cache.transpose(1, 0, 2).reshape(row_count, local_heads, -1)
    return (attended, cache)


def solution(mesh):
    return jax.shard_map(
        functools.partial(local, *(mesh.shape[a] for a in ("seq", "grp", "head", "hold"))),
        mesh=mesh,
        in_specs=(
            P("grp"),
            P("grp"),
            P(("grp", "seq"), None),
            P("seq", ("head", "hold"), None),
            P("seq", ("head", "hold"), None),
            P(("grp", "seq"), ("head", "hold"), None),
        ),
        out_specs=(
            P(("grp", "seq"), ("head", "hold"), None),
            P(("grp", "seq"), ("head", "hold"), None),
        ),
        check_vma=False,
    )
```

```python
import functools
import math

import jax
import jax.numpy as jnp
from jax import lax
from jax.experimental import pallas as pl
from jax.experimental.pallas import tpu as pltpu
from jax.sharding import PartitionSpec as P

CH = 256
MESH = pl.DeviceIdType.MESH

theta_base = 500000.0
lowest = -1e30


def rotary_tables(positions, head_width):
    half_width = head_width // 2
    frequency = theta_base ** (
        -(jnp.arange(half_width, dtype=jnp.float32) * 2.0) / head_width
    )
    angles = positions.astype(jnp.float32)[:, None] * frequency[None, :]
    cosine, sine = jnp.cos(angles), jnp.sin(angles)
    return jnp.concatenate([cosine, cosine], -1), jnp.concatenate([-sine, sine], -1)


def kernel(
    n, groups, head_dev, hold_dev, local_heads, group_size,
    hidden_hbm, own_kv, own_q, stored_hbm, cos_ref, sin_ref, qpos_ref, done_ref, done_row, kpos_ref,
    out_ref, cache_ref,
    hid, wbuf, kvbuf, stored, gout, turned_values, acc,
    hid_sem, st_sem, own_sem, up_send, down_send, z_recv, y_send, y_recv,
    kv_up, kv_down, kv_recv,
    lend_send, lend_recv, x_send, x_recv, mate_send, mate_recv,
    st_send, st_recv, back_send, back_recv, ret_send, ret_recv,
):
    s = lax.axis_index("seq")
    g = lax.axis_index("grp")
    hx = lax.axis_index("head")
    hc = lax.axis_index("hold")
    planes, rows, width = cache_ref.shape
    heads = out_ref.shape[0]
    chunks = planes + heads
    depth = own_kv.shape[0]
    part = depth if groups == 1 else (depth // 16) * 9
    rest_part = depth - part
    subs = lend_send.shape[0]
    sub_width = hid.shape[1] // subs
    lent_rows = rows // (head_dev * hold_dev)
    idle = (s == 0) | (s == n - 1)
    host = (s == 1) | (s == n - 2)
    partner = jnp.where(s == 0, 1, n - 2)
    guest = jnp.where(s == 1, 0, n - 1)
    has_up, has_down = (s < n - 2) & ~idle, (s > 1) & ~idle
    near_up, near_down = s + 1 < n, s > 0
    row_groups = jnp.where(idle, 0, jnp.where(host, 2, 1))

    barrier = pltpu.get_barrier_semaphore()

    def greet(device):
        pl.semaphore_signal(barrier, inc=1, device_id=device, device_id_type=MESH)

    @pl.when(near_up)
    def _():
        greet({"seq": s + 1})

    @pl.when(near_down)
    def _():
        greet({"seq": s - 1})

    for k in range(1, groups):
        greet({"grp": lax.rem(g + k, groups)})
    for k in range(1, head_dev):
        greet({"head": lax.rem(hx + k, head_dev)})
    for k in range(1, hold_dev):
        greet({"hold": lax.rem(hc + k, hold_dev)})

    def columns(c):
        return pl.ds(pl.multiple_of(c * width, width), width)

    def row_range(i):
        return pl.ds(pl.multiple_of(i * rows, rows), rows)

    hid_copy = pltpu.make_async_copy(hidden_hbm, hid.at[pl.ds(0, rows), :], hid_sem)
    hid_copy.start()
    st_copy = pltpu.make_async_copy(stored_hbm, stored.at[:, pl.ds(0, rows), :], st_sem)
    st_copy.start()

    def own_copy(c):
        own = own_kv.at[:, columns(c)] if c < planes else own_q.at[:, columns(c - planes)]
        return pltpu.make_async_copy(
            own, wbuf.at[c, pl.ds(pl.multiple_of(s * depth, depth), depth), :], own_sem.at[c]
        )

    for c in range(chunks):
        own_copy(c).start()
    pl.semaphore_wait(
        barrier,
        jnp.where(near_up, 1, 0) + jnp.where(near_down, 1, 0)
        + (groups - 1 + head_dev - 1 + hold_dev - 1),
    )

    def piece(c, o):
        return wbuf.at[c, pl.ds(pl.multiple_of(o * depth + g * rest_part, 16), part), :]

    def side_piece(c, o, sender):
        return wbuf.at[c, pl.ds(pl.multiple_of(o * depth + sender * part, 16), rest_part), :]

    def kv_piece(j, o):
        return kvbuf.at[j, row_range(o), :]

    def remote(src, dst, send_sem, recv_sem, **device):
        return pltpu.make_async_remote_copy(
            src_ref=src, dst_ref=dst, send_sem=send_sem, recv_sem=recv_sem,
            device_id=device, device_id_type=MESH,
        )

    def up_copy(c, o, src=None):
        src = piece(c, o) if src is None else src
        return remote(src, piece(c, o), up_send.at[c, o], z_recv.at[c, o], seq=s + 1)

    def down_copy(c, o, src=None):
        src = piece(c, o) if src is None else src
        return remote(src, piece(c, o), down_send.at[c, o], z_recv.at[c, o], seq=s - 1)

    def side_copy(c, o, sender, target):
        at = side_piece(c, o, sender)
        return remote(at, at, y_send.at[c, o], y_recv.at[c, o], grp=target)

    def kv_up_copy(j, o):
        at = kv_piece(j, o)
        return remote(at, at, kv_up.at[j, o], kv_recv.at[j, o], seq=s + 1)

    def kv_down_copy(j, o):
        at = kv_piece(j, o)
        return remote(at, at, kv_down.at[j, o], kv_recv.at[j, o], seq=s - 1)

    def hid_piece(x, h, k):
        start = rows + (x * hold_dev + h) * lent_rows
        return hid.at[
            pl.ds(pl.multiple_of(start, 16), lent_rows), pl.ds(k * sub_width, sub_width)
        ]

    def lend_copy(k):
        start = (hx * hold_dev + hc) * lent_rows
        src = hidden_hbm.at[
            pl.ds(pl.multiple_of(start, 16), lent_rows), pl.ds(k * sub_width, sub_width)
        ]
        return remote(src, hid_piece(hx, hc, k), lend_send.at[k], lend_recv.at[k], seq=partner)

    def x_copy(k, x, target):
        at = hid_piece(x, hc, k)
        return remote(at, at, x_send.at[k, target], x_recv.at[k, x], head=target)

    def mate_copy(k, x, h, target):
        at = hid_piece(x, h, k)
        return remote(at, at, mate_send.at[k, x, target], mate_recv.at[k, x, h], hold=target)

    def st_lend():
        return remote(
            stored_hbm, stored.at[:, pl.ds(rows, rows), :], st_send, st_recv, seq=partner
        )

    def back_copy(j):
        return remote(
            kv_piece(j, guest), cache_ref.at[j], back_send.at[j], back_recv.at[j], seq=guest
        )

    def ret_copy(q):
        return remote(gout.at[q], out_ref.at[q], ret_send.at[q], ret_recv.at[q], seq=guest)

    def send_own(c):
        at = pl.ds(pl.multiple_of(g * rest_part, 16), part)
        src = own_kv.at[at, columns(c)] if c < planes else own_q.at[at, columns(c - planes)]

        @pl.when(has_up)
        def _():
            up_copy(c, s, src).start()

        @pl.when(has_down)
        def _():
            down_copy(c, s, src).start()

    def send_own_q(q):
        at = pl.ds(pl.multiple_of(g * rest_part, 16), part)
        src = own_q.at[at, columns(q)]

        @pl.when(has_up)
        def _():
            up_copy(planes + q, s, src).start()

        @pl.when(has_down)
        def _():
            down_copy(planes + q, s, src).start()

    def spread(c, o):
        for k in range(1, groups):
            side_copy(c, o, g, lax.rem(g + k, groups)).start()

    def forward(c, inner_done=False):
        def hop(d, _):
            lo, hi = s - d, s + d
            first = (d == 1) & host & inner_done

            @pl.when((lo >= 0) & ~idle & ~(first & (s == n - 2)))
            def _():
                up_copy(c, lo).wait_recv()

                @pl.when(has_up)
                def _():
                    up_copy(c, lo).start()

                spread(c, lo)

            @pl.when((hi < n) & ~idle & ~(first & (s == 1)))
            def _():
                down_copy(c, hi).wait_recv()

                @pl.when(has_down)
                def _():
                    down_copy(c, hi).start()

                spread(c, hi)

            return 0

        lax.fori_loop(1, n, hop, 0)

    def inner_first(c):
        o = jnp.where(s == 1, s + 1, s - 1)
        down_copy(c, o).wait_recv()
        spread(c, o)

    def kv_hop(j, d):
        lo, hi = s - d, s + d

        @pl.when((lo >= 0) & (s > 1) & ~idle)
        def _():
            kv_up_copy(j, lo).wait_recv()

            @pl.when(has_up)
            def _():
                kv_up_copy(j, lo).start()

        @pl.when((hi < n) & (s < n - 2) & ~idle)
        def _():
            kv_down_copy(j, hi).wait_recv()

            @pl.when(has_down)
            def _():
                kv_down_copy(j, hi).start()

    def gather_side(c):
        def each(o, _):
            @pl.when((o != s) & ~idle)
            def _():
                for k in range(1, groups):
                    side_copy(c, o, lax.rem(g + k, groups), g).wait_recv()

            return 0

        lax.fori_loop(0, n, each, 0)

    def project(c, r):
        acc[...] = jnp.zeros_like(acc)

        def add(o, _):
            at = pl.ds(pl.multiple_of(o * depth, depth), depth)
            pair = jnp.concatenate([wbuf[c, at, :], wbuf[c + 1, at, :]], -1)
            acc[...] += jnp.dot(
                hid[row_range(r), at], pair, preferred_element_type=jnp.float32
            )
            return 0

        lax.fori_loop(0, n, add, 0)

    def rotated(raw, r):
        half = width // 2
        turned = jnp.concatenate([raw[:, half:], raw[:, :half]], -1)
        return raw * cos_ref[row_range(r), :] + turned * sin_ref[row_range(r), :]

    def make_planes(h, r):
        project(2 * h, r)
        o = jnp.where(r == 0, s, guest)
        for i in range(2):
            c = 2 * h + i
            raw = acc[:, i * width:(i + 1) * width]
            fresh = (rotated(raw, r) if i == 0 else raw).astype(jnp.bfloat16)
            fresh = jnp.where(done_ref[row_range(r), :] > 0, fresh, stored[c, row_range(r), :])
            kvbuf[c, row_range(o), :] = fresh

            @pl.when(r == 0)
            def _():
                cache_ref[c] = fresh

            @pl.when(r == 1)
            def _():
                back_copy(c).start()

            @pl.when(has_up)
            def _():
                kv_up_copy(c, o).start()

            @pl.when(has_down)
            def _():
                kv_down_copy(c, o).start()

    row_block = 256
    scale = width ** (-0.5) * math.log2(math.e)

    def attend(q, r, i):
        head = q // group_size

        def block(b, _):
            at = pl.ds(pl.multiple_of(b * row_block, row_block), row_block)
            full = pl.ds(pl.multiple_of(r * rows + b * row_block, row_block), row_block)
            raw = acc[at, i * width:(i + 1) * width]
            half = width // 2
            turned = jnp.concatenate([raw[:, half:], raw[:, :half]], -1)
            queries = (raw * cos_ref[full, :] + turned * sin_ref[full, :]).astype(jnp.bfloat16)
            scores = lax.dot_general(
                kvbuf[2 * head], queries, (((1,), (1,)), ((), ())),
                preferred_element_type=jnp.float32,
            ) * scale
            key_pos = jnp.concatenate([kpos_ref[...]] * (row_block // width), -1)
            scores = jnp.where(key_pos <= qpos_ref[:, full], scores, lowest)
            top = scores.max(0, keepdims=True)
            weights = jnp.exp2(scores - top)
            total = weights.sum(0, keepdims=True)
            mixed = jnp.dot(
                turned_values[...], weights.astype(jnp.bfloat16),
                preferred_element_type=jnp.float32,
            ) / total
            mixed = jnp.where(done_row[:, full] > 0, mixed, 0.0).T.astype(jnp.bfloat16)

            @pl.when(r == 0)
            def _():
                out_ref[q, at, :] = mixed

            @pl.when(r == 1)
            def _():
                gout[q, at, :] = mixed

            return 0

        lax.fori_loop(0, rows // row_block, block, 0)

        @pl.when(r == 1)
        def _():
            ret_copy(q).start()

    for c in range(planes):
        send_own(c)

    @pl.when(idle)
    def _():
        def own_to_partner(c):
            at = pl.ds(pl.multiple_of(g * rest_part, 16), part)
            src = own_kv.at[at, columns(c)] if c < planes else own_q.at[at, columns(c - planes)]

            @pl.when(s == 0)
            def _():
                up_copy(c, s, src).start()

            @pl.when(s == n - 1)
            def _():
                down_copy(c, s, src).start()

        def own_sent(c):
            @pl.when(s == 0)
            def _():
                up_copy(c, s).wait_send()

            @pl.when(s == n - 1)
            def _():
                down_copy(c, s).wait_send()

        order = [(functools.partial(own_to_partner, c), functools.partial(own_sent, c))
                 for c in range(chunks)]
        lent = [(lend_copy(k).start, lend_copy(k).wait_send) for k in range(subs)]
        lent.append((st_lend().start, st_lend().wait_send))
        order = order[:planes] + lent + order[planes:]
        in_flight = 3
        for i, (start, _) in enumerate(order):
            if i >= in_flight:
                order[i - in_flight][1]()
            start()
        for _, sent in order[-in_flight:]:
            sent()

    for c in range(chunks):
        own_copy(c).wait()
    hid_copy.wait()
    st_copy.wait()

    def early(t, _):
        @pl.when(t < local_heads)
        def _():
            forward(2 * t)
            forward(2 * t + 1)

            def more(i, _):
                send_own_q(t * group_size + i)
                return 0

            lax.fori_loop(0, group_size, more, 0)

        @pl.when(t >= 1)
        def _():
            gather_side(2 * t - 2)
            gather_side(2 * t - 1)

            @pl.when(~idle)
            def _():
                make_planes(t - 1, 0)

        return 0

    lax.fori_loop(0, local_heads + 1, early, 0)

    @pl.when(host)
    def _():
        for k in range(subs):
            lend_copy_in = remote(
                hid_piece(hx, hc, k), hid_piece(hx, hc, k),
                lend_send.at[k], lend_recv.at[k], seq=guest,
            )
            lend_copy_in.wait_recv()
            for i in range(1, head_dev):
                x_copy(k, hx, lax.rem(hx + i, head_dev)).start()
            for i in range(1, hold_dev):
                mate_copy(k, hx, hc, lax.rem(hc + i, hold_dev)).start()
            if k < heads:
                inner_first(planes + k)
        for k in range(subs):
            for i in range(1, head_dev):
                x = lax.rem(hx + i, head_dev)
                x_copy(k, x, hx).wait_recv()
                for m in range(1, hold_dev):
                    mate_copy(k, x, hc, lax.rem(hc + m, hold_dev)).start()
        for k in range(subs):
            for x in range(head_dev):
                for m in range(1, hold_dev):
                    mate_copy(k, x, lax.rem(hc + m, hold_dev), hc).wait_recv()
        st_in = stored.at[:, pl.ds(rows, rows), :]
        remote(st_in, st_in, st_send, st_recv, seq=guest).wait_recv()

        def guest_planes(h, _):
            make_planes(h, 1)
            return 0

        lax.fori_loop(0, local_heads, guest_planes, 0)

        def inner_rest(c, _):
            inner_first(c)
            return 0

        lax.fori_loop(planes + subs, chunks, inner_rest, 0)

    def late(t, _):
        @pl.when(t < heads // 2)
        def _():
            forward(planes + 2 * t, True)
            forward(planes + 2 * t + 1, True)

        @pl.when(t >= 1)
        def _():
            q = 2 * (t - 1)
            c = planes + q
            gather_side(c)
            gather_side(c + 1)

            @pl.when((lax.rem(q, group_size) == 0) & ~idle)
            def _():
                head = q // group_size

                def rest(d, _):
                    kv_hop(2 * head, d)
                    kv_hop(2 * head + 1, d)
                    return 0

                lax.fori_loop(1, n, rest, 0)
                turned_values[...] = kvbuf[2 * head + 1].T

            def each(r, _):
                project(c, r)
                attend(q, r, 0)
                attend(q + 1, r, 1)
                return 0

            lax.fori_loop(0, row_groups, each, 0)

        return 0

    lax.fori_loop(0, heads // 2 + 1, late, 0)

    def drain(c, _):
        def each(o, _):
            @pl.when(has_up & (o <= s))
            def _():
                up_copy(c, o).wait_send()

            @pl.when(has_down & (o >= s))
            def _():
                down_copy(c, o).wait_send()

            @pl.when((o != s) & ~idle)
            def _():
                for k in range(1, groups):
                    side_copy(c, o, g, lax.rem(g + k, groups)).wait_send()

            return 0

        lax.fori_loop(0, n, each, 0)
        return 0

    lax.fori_loop(0, chunks, drain, 0)

    def kv_drain(j, _):
        def each(o, _):
            @pl.when(has_up & (o <= s))
            def _():
                kv_up_copy(j, o).wait_send()

            @pl.when(has_down & (o >= s))
            def _():
                kv_down_copy(j, o).wait_send()

            return 0

        lax.fori_loop(0, n, each, 0)

        @pl.when(host)
        def _():
            back_copy(j).wait_send()

        @pl.when(idle)
        def _():
            at = cache_ref.at[j]
            remote(at, at, back_send.at[j], back_recv.at[j], seq=partner).wait_recv()

        return 0

    lax.fori_loop(0, planes, kv_drain, 0)

    @pl.when(host)
    def _():
        for k in range(subs):
            for i in range(1, head_dev):
                x_copy(k, hx, lax.rem(hx + i, head_dev)).wait_send()
            for x in range(head_dev):
                for m in range(1, hold_dev):
                    mate_copy(k, x, hc, lax.rem(hc + m, hold_dev)).wait_send()
        for q in range(heads):
            ret_copy(q).wait_send()

    @pl.when(idle)
    def _():
        for q in range(heads):
            at = out_ref.at[q]
            remote(at, at, ret_send.at[q], ret_recv.at[q], seq=partner).wait_recv()


def local(n, groups, head_dev, hold_dev, meet_span, span_map, hidden, w_query, w_keyval, stored_kv):
    row_count, features = hidden.shape
    span_count = span_map.shape[0]
    depth, local_heads = w_query.shape[:2]
    head_width = stored_kv.shape[2] // 2
    group_size = w_query.shape[2] // head_width
    span_len = CH
    slots_dev = row_count // span_len
    planes, heads = 2 * local_heads, local_heads * group_size
    chunks = planes + heads
    offsets = jnp.arange(span_len, dtype=jnp.int32)
    key_pos = (span_map[:, None] * span_len + offsets[None, :]).reshape(-1, 1)
    key_pos = jnp.broadcast_to(key_pos, (key_pos.shape[0], head_width))
    seq_index = lax.axis_index("seq")
    guest = jnp.where(seq_index == 1, 0, n - 1)
    my_spans = jnp.concatenate(
        [
            lax.dynamic_slice_in_dim(span_map, index * slots_dev, slots_dev, 0)
            for index in (seq_index, guest)
        ]
    )
    positions = (my_spans[:, None] * span_len + offsets[None, :]).reshape(-1)
    computed_slot = (my_spans < meet_span[0]) | (my_spans == span_count - 1)
    done = jnp.repeat(computed_slot, span_len).astype(jnp.int32)[:, None]
    cosine, sine = rotary_tables(positions, head_width)
    own_kv = w_keyval.reshape(depth, planes * head_width)
    own_q = w_query.reshape(depth, heads * head_width)
    stored = stored_kv.reshape(row_count, planes, head_width).transpose(1, 0, 2)
    subs = 4
    vmem = pl.BlockSpec(memory_space=pltpu.VMEM)
    hbm = pl.BlockSpec(memory_space=pl.ANY)
    dma = pltpu.SemaphoreType.DMA
    attended, cache = pl.pallas_call(
        functools.partial(kernel, n, groups, head_dev, hold_dev, local_heads, group_size),
        out_shape=(
            jax.ShapeDtypeStruct((heads, row_count, head_width), jnp.bfloat16),
            jax.ShapeDtypeStruct((planes, row_count, head_width), jnp.bfloat16),
        ),
        in_specs=[hbm] * 4 + [vmem] * 6,
        out_specs=(vmem, vmem),
        scratch_shapes=[
            pltpu.VMEM((2 * row_count, features), jnp.bfloat16),
            pltpu.VMEM((chunks, features, head_width), jnp.bfloat16),
            pltpu.VMEM((planes, n * row_count, head_width), jnp.bfloat16),
            pltpu.VMEM((planes, 2 * row_count, head_width), jnp.bfloat16),
            pltpu.VMEM((heads, row_count, head_width), jnp.bfloat16),
            pltpu.VMEM((head_width, n * row_count), jnp.bfloat16),
            pltpu.VMEM((row_count, 2 * head_width), jnp.float32),
            dma,
            dma,
            dma((chunks,)),
        ]
        + [dma((chunks, n))] * 5
        + [dma((planes, n))] * 3
        + [dma((subs,))] * 2
        + [dma((subs, head_dev))] * 2
        + [dma((subs, head_dev, hold_dev))] * 2
        + [dma] * 2
        + [dma((planes,))] * 2
        + [dma((heads,))] * 2,
        compiler_params=pltpu.CompilerParams(
            collective_id=0, has_side_effects=True, vmem_limit_bytes=60 * 1024 * 1024
        ),
    )(hidden, own_kv, own_q, stored, cosine, sine, positions[None, :], done, done.reshape(1, -1), key_pos)
    attended = attended.transpose(1, 0, 2).reshape(row_count, local_heads, -1)
    cache = cache.transpose(1, 0, 2).reshape(row_count, local_heads, -1)
    return (attended, cache)


def solution(mesh):
    return jax.shard_map(
        functools.partial(local, *(mesh.shape[a] for a in ("seq", "grp", "head", "hold"))),
        mesh=mesh,
        in_specs=(
            P("grp"),
            P("grp"),
            P(("grp", "seq"), None),
            P("seq", ("head", "hold"), None),
            P("seq", ("head", "hold"), None),
            P(("grp", "seq"), ("head", "hold"), None),
        ),
        out_specs=(
            P(("grp", "seq"), ("head", "hold"), None),
            P(("grp", "seq"), ("head", "hold"), None),
        ),
        check_vma=False,
    )
```

```python
import functools
import math

import jax
import jax.numpy as jnp
from jax import lax
from jax.experimental import pallas as pl
from jax.experimental.pallas import tpu as pltpu
from jax.sharding import PartitionSpec as P

CH = 256
MESH = pl.DeviceIdType.MESH

theta_base = 500000.0
lowest = -1e30


def rotary_tables(positions, head_width):
    half_width = head_width // 2
    frequency = theta_base ** (
        -(jnp.arange(half_width, dtype=jnp.float32) * 2.0) / head_width
    )
    angles = positions.astype(jnp.float32)[:, None] * frequency[None, :]
    cosine, sine = jnp.cos(angles), jnp.sin(angles)
    return jnp.concatenate([cosine, cosine], -1), jnp.concatenate([-sine, sine], -1)


def kernel(
    n, groups, head_dev, hold_dev, local_heads, group_size,
    hidden_hbm, own_kv, own_q, stored_hbm, cos_ref, sin_ref, qpos_ref, done_ref, done_row, kpos_ref,
    out_ref, cache_ref,
    hid, wbuf, kvbuf, stored, gout, turned_values, acc,
    hid_sem, st_sem, own_sem, up_send, down_send, z_recv, y_send, y_recv,
    kv_up, kv_down, kv_recv,
    lend_send, lend_recv, x_send, x_recv, mate_send, mate_recv,
    st_send, st_recv, back_send, back_recv, ret_send, ret_recv,
):
    s = lax.axis_index("seq")
    g = lax.axis_index("grp")
    hx = lax.axis_index("head")
    hc = lax.axis_index("hold")
    planes, rows, width = cache_ref.shape
    heads = out_ref.shape[0]
    chunks = planes + heads
    depth = own_kv.shape[0]
    part = depth if groups == 1 else (depth // 16) * 9
    rest_part = depth - part
    subs = lend_send.shape[0]
    sub_width = hid.shape[1] // subs
    lent_rows = rows // (head_dev * hold_dev)
    idle = (s == 0) | (s == n - 1)
    host = (s == 1) | (s == n - 2)
    partner = jnp.where(s == 0, 1, n - 2)
    guest = jnp.where(s == 1, 0, n - 1)
    has_up, has_down = (s < n - 2) & ~idle, (s > 1) & ~idle
    near_up, near_down = s + 1 < n, s > 0
    row_groups = jnp.where(idle, 0, jnp.where(host, 2, 1))

    barrier = pltpu.get_barrier_semaphore()

    def greet(device):
        pl.semaphore_signal(barrier, inc=1, device_id=device, device_id_type=MESH)

    @pl.when(near_up)
    def _():
        greet({"seq": s + 1})

    @pl.when(near_down)
    def _():
        greet({"seq": s - 1})

    for k in range(1, groups):
        greet({"grp": lax.rem(g + k, groups)})
    for k in range(1, head_dev):
        greet({"head": lax.rem(hx + k, head_dev)})
    for k in range(1, hold_dev):
        greet({"hold": lax.rem(hc + k, hold_dev)})

    def columns(c):
        return pl.ds(pl.multiple_of(c * width, width), width)

    def row_range(i):
        return pl.ds(pl.multiple_of(i * rows, rows), rows)

    hid_copy = pltpu.make_async_copy(hidden_hbm, hid.at[pl.ds(0, rows), :], hid_sem)
    hid_copy.start()
    st_copy = pltpu.make_async_copy(stored_hbm, stored.at[:, pl.ds(0, rows), :], st_sem)
    st_copy.start()

    def own_copy(c):
        own = own_kv.at[:, columns(c)] if c < planes else own_q.at[:, columns(c - planes)]
        return pltpu.make_async_copy(
            own, wbuf.at[c, pl.ds(pl.multiple_of(s * depth, depth), depth), :], own_sem.at[c]
        )

    for c in range(chunks):
        own_copy(c).start()
    pl.semaphore_wait(
        barrier,
        jnp.where(near_up, 1, 0) + jnp.where(near_down, 1, 0)
        + (groups - 1 + head_dev - 1 + hold_dev - 1),
    )

    def piece(c, o):
        return wbuf.at[c, pl.ds(pl.multiple_of(o * depth + g * rest_part, 16), part), :]

    def side_piece(c, o, sender):
        return wbuf.at[c, pl.ds(pl.multiple_of(o * depth + sender * part, 16), rest_part), :]

    def kv_piece(j, o):
        return kvbuf.at[j, row_range(o), :]

    def remote(src, dst, send_sem, recv_sem, **device):
        return pltpu.make_async_remote_copy(
            src_ref=src, dst_ref=dst, send_sem=send_sem, recv_sem=recv_sem,
            device_id=device, device_id_type=MESH,
        )

    def up_copy(c, o, src=None):
        src = piece(c, o) if src is None else src
        return remote(src, piece(c, o), up_send.at[c, o], z_recv.at[c, o], seq=s + 1)

    def down_copy(c, o, src=None):
        src = piece(c, o) if src is None else src
        return remote(src, piece(c, o), down_send.at[c, o], z_recv.at[c, o], seq=s - 1)

    def side_copy(c, o, sender, target):
        at = side_piece(c, o, sender)
        return remote(at, at, y_send.at[c, o], y_recv.at[c, o], grp=target)

    def kv_up_copy(j, o):
        at = kv_piece(j, o)
        return remote(at, at, kv_up.at[j, o], kv_recv.at[j, o], seq=s + 1)

    def kv_down_copy(j, o):
        at = kv_piece(j, o)
        return remote(at, at, kv_down.at[j, o], kv_recv.at[j, o], seq=s - 1)

    def hid_piece(x, h, k):
        start = rows + (x * hold_dev + h) * lent_rows
        return hid.at[
            pl.ds(pl.multiple_of(start, 16), lent_rows), pl.ds(k * sub_width, sub_width)
        ]

    def lend_copy(k):
        start = (hx * hold_dev + hc) * lent_rows
        src = hidden_hbm.at[
            pl.ds(pl.multiple_of(start, 16), lent_rows), pl.ds(k * sub_width, sub_width)
        ]
        return remote(src, hid_piece(hx, hc, k), lend_send.at[k], lend_recv.at[k], seq=partner)

    def x_copy(k, x, target):
        at = hid_piece(x, hc, k)
        return remote(at, at, x_send.at[k, target], x_recv.at[k, x], head=target)

    def mate_copy(k, x, h, target):
        at = hid_piece(x, h, k)
        return remote(at, at, mate_send.at[k, x, target], mate_recv.at[k, x, h], hold=target)

    def st_lend():
        return remote(
            stored_hbm, stored.at[:, pl.ds(rows, rows), :], st_send, st_recv, seq=partner
        )

    def back_copy(j):
        return remote(
            kv_piece(j, guest), cache_ref.at[j], back_send.at[j], back_recv.at[j], seq=guest
        )

    def ret_copy(q):
        return remote(gout.at[q], out_ref.at[q], ret_send.at[q], ret_recv.at[q], seq=guest)

    def send_own(c):
        at = pl.ds(pl.multiple_of(g * rest_part, 16), part)
        src = own_kv.at[at, columns(c)] if c < planes else own_q.at[at, columns(c - planes)]

        @pl.when(has_up)
        def _():
            up_copy(c, s, src).start()

        @pl.when(has_down)
        def _():
            down_copy(c, s, src).start()

    def send_own_q(q):
        at = pl.ds(pl.multiple_of(g * rest_part, 16), part)
        src = own_q.at[at, columns(q)]

        @pl.when(has_up)
        def _():
            up_copy(planes + q, s, src).start()

        @pl.when(has_down)
        def _():
            down_copy(planes + q, s, src).start()

    def spread(c, o):
        for k in range(1, groups):
            side_copy(c, o, g, lax.rem(g + k, groups)).start()

    def forward(c, inner_done=False):
        def hop(d, _):
            lo, hi = s - d, s + d
            first = (d == 1) & host & inner_done

            @pl.when((lo >= 0) & ~idle & ~first)
            def _():
                up_copy(c, lo).wait_recv()

                @pl.when(has_up)
                def _():
                    up_copy(c, lo).start()

                spread(c, lo)

            @pl.when((hi < n) & ~idle & ~first)
            def _():
                down_copy(c, hi).wait_recv()

                @pl.when(has_down)
                def _():
                    down_copy(c, hi).start()

                spread(c, hi)

            return 0

        lax.fori_loop(1, n, hop, 0)

    def outer_first(c):
        o = guest
        up_copy(c, o).wait_recv()

        @pl.when(s == 1)
        def _():
            up_copy(c, o).start()

        @pl.when(s == n - 2)
        def _():
            down_copy(c, o).start()

        spread(c, o)

    def inner_first(c):
        o = jnp.where(s == 1, s + 1, s - 1)
        down_copy(c, o).wait_recv()
        spread(c, o)

    def kv_hop(j, d):
        lo, hi = s - d, s + d

        @pl.when((lo >= 0) & (s > 1) & ~idle)
        def _():
            kv_up_copy(j, lo).wait_recv()

            @pl.when(has_up)
            def _():
                kv_up_copy(j, lo).start()

        @pl.when((hi < n) & (s < n - 2) & ~idle)
        def _():
            kv_down_copy(j, hi).wait_recv()

            @pl.when(has_down)
            def _():
                kv_down_copy(j, hi).start()

    def gather_side(c):
        def each(o, _):
            @pl.when((o != s) & ~idle)
            def _():
                for k in range(1, groups):
                    side_copy(c, o, lax.rem(g + k, groups), g).wait_recv()

            return 0

        lax.fori_loop(0, n, each, 0)

    def project(c, r):
        acc[...] = jnp.zeros_like(acc)

        def add(o, _):
            at = pl.ds(pl.multiple_of(o * depth, depth), depth)
            pair = jnp.concatenate([wbuf[c, at, :], wbuf[c + 1, at, :]], -1)
            acc[...] += jnp.dot(
                hid[row_range(r), at], pair, preferred_element_type=jnp.float32
            )
            return 0

        lax.fori_loop(0, n, add, 0)

    def rotated(raw, r):
        half = width // 2
        turned = jnp.concatenate([raw[:, half:], raw[:, :half]], -1)
        return raw * cos_ref[row_range(r), :] + turned * sin_ref[row_range(r), :]

    def make_planes(h, r):
        project(2 * h, r)
        o = jnp.where(r == 0, s, guest)
        for i in range(2):
            c = 2 * h + i
            raw = acc[:, i * width:(i + 1) * width]
            fresh = (rotated(raw, r) if i == 0 else raw).astype(jnp.bfloat16)
            fresh = jnp.where(done_ref[row_range(r), :] > 0, fresh, stored[c, row_range(r), :])
            kvbuf[c, row_range(o), :] = fresh

            @pl.when(r == 0)
            def _():
                cache_ref[c] = fresh

            @pl.when(r == 1)
            def _():
                back_copy(c).start()

            @pl.when(has_up)
            def _():
                kv_up_copy(c, o).start()

            @pl.when(has_down)
            def _():
                kv_down_copy(c, o).start()

    row_block = 256
    scale = width ** (-0.5) * math.log2(math.e)

    def attend(q, r, i):
        head = q // group_size

        def block(b, _):
            at = pl.ds(pl.multiple_of(b * row_block, row_block), row_block)
            full = pl.ds(pl.multiple_of(r * rows + b * row_block, row_block), row_block)
            raw = acc[at, i * width:(i + 1) * width]
            half = width // 2
            turned = jnp.concatenate([raw[:, half:], raw[:, :half]], -1)
            queries = (raw * cos_ref[full, :] + turned * sin_ref[full, :]).astype(jnp.bfloat16)
            scores = lax.dot_general(
                kvbuf[2 * head], queries, (((1,), (1,)), ((), ())),
                preferred_element_type=jnp.float32,
            ) * scale
            key_pos = jnp.concatenate([kpos_ref[...]] * (row_block // width), -1)
            scores = jnp.where(key_pos <= qpos_ref[:, full], scores, lowest)
            top = scores.max(0, keepdims=True)
            weights = jnp.exp2(scores - top)
            total = weights.sum(0, keepdims=True)
            mixed = jnp.dot(
                turned_values[...], weights.astype(jnp.bfloat16),
                preferred_element_type=jnp.float32,
            ) / total
            mixed = jnp.where(done_row[:, full] > 0, mixed, 0.0).T.astype(jnp.bfloat16)

            @pl.when(r == 0)
            def _():
                out_ref[q, at, :] = mixed

            @pl.when(r == 1)
            def _():
                gout[q, at, :] = mixed

            return 0

        lax.fori_loop(0, rows // row_block, block, 0)

        @pl.when(r == 1)
        def _():
            ret_copy(q).start()

    for c in range(planes):
        send_own(c)

    @pl.when(idle)
    def _():
        def own_to_partner(c):
            at = pl.ds(pl.multiple_of(g * rest_part, 16), part)
            src = own_kv.at[at, columns(c)] if c < planes else own_q.at[at, columns(c - planes)]

            @pl.when(s == 0)
            def _():
                up_copy(c, s, src).start()

            @pl.when(s == n - 1)
            def _():
                down_copy(c, s, src).start()

        def own_sent(c):
            @pl.when(s == 0)
            def _():
                up_copy(c, s).wait_send()

            @pl.when(s == n - 1)
            def _():
                down_copy(c, s).wait_send()

        order = [(functools.partial(own_to_partner, c), functools.partial(own_sent, c))
                 for c in range(chunks)]
        lent = [(lend_copy(k).start, lend_copy(k).wait_send) for k in range(subs)]
        lent.append((st_lend().start, st_lend().wait_send))
        order = order[:planes] + lent + order[planes:]
        in_flight = 3
        for i, (start, _) in enumerate(order):
            if i >= in_flight:
                order[i - in_flight][1]()
            start()
        for _, sent in order[-in_flight:]:
            sent()

    for c in range(chunks):
        own_copy(c).wait()
    hid_copy.wait()
    st_copy.wait()

    def early(t, _):
        @pl.when(t < local_heads)
        def _():
            forward(2 * t)
            forward(2 * t + 1)

            def more(i, _):
                send_own_q(t * group_size + i)
                return 0

            lax.fori_loop(0, group_size, more, 0)

        @pl.when(t >= 1)
        def _():
            gather_side(2 * t - 2)
            gather_side(2 * t - 1)

            @pl.when(~idle)
            def _():
                make_planes(t - 1, 0)

        return 0

    lax.fori_loop(0, local_heads + 1, early, 0)

    @pl.when(host)
    def _():
        for k in range(subs):
            lend_copy_in = remote(
                hid_piece(hx, hc, k), hid_piece(hx, hc, k),
                lend_send.at[k], lend_recv.at[k], seq=guest,
            )
            lend_copy_in.wait_recv()
            for i in range(1, head_dev):
                x_copy(k, hx, lax.rem(hx + i, head_dev)).start()
            for i in range(1, hold_dev):
                mate_copy(k, hx, hc, lax.rem(hc + i, hold_dev)).start()
            if k < heads:
                inner_first(planes + k)
        for k in range(subs):
            for i in range(1, head_dev):
                x = lax.rem(hx + i, head_dev)
                x_copy(k, x, hx).wait_recv()
                for m in range(1, hold_dev):
                    mate_copy(k, x, hc, lax.rem(hc + m, hold_dev)).start()
        for k in range(subs):
            for x in range(head_dev):
                for m in range(1, hold_dev):
                    mate_copy(k, x, lax.rem(hc + m, hold_dev), hc).wait_recv()
        st_in = stored.at[:, pl.ds(rows, rows), :]
        remote(st_in, st_in, st_send, st_recv, seq=guest).wait_recv()

        def guest_planes(h, _):
            make_planes(h, 1)
            return 0

        lax.fori_loop(0, local_heads, guest_planes, 0)
        outer_first(planes)
        outer_first(planes + 1)

        def inner_rest(c, _):
            inner_first(c)
            return 0

        lax.fori_loop(planes + subs, chunks, inner_rest, 0)

    def late(t, _):
        @pl.when((t + 1 < heads // 2) & host)
        def _():
            outer_first(planes + 2 * t + 2)
            outer_first(planes + 2 * t + 3)

        @pl.when(t < heads // 2)
        def _():
            forward(planes + 2 * t, True)
            forward(planes + 2 * t + 1, True)

        @pl.when(t >= 1)
        def _():
            q = 2 * (t - 1)
            c = planes + q
            gather_side(c)
            gather_side(c + 1)

            @pl.when((lax.rem(q, group_size) == 0) & ~idle)
            def _():
                head = q // group_size

                def rest(d, _):
                    kv_hop(2 * head, d)
                    kv_hop(2 * head + 1, d)
                    return 0

                lax.fori_loop(1, n, rest, 0)
                turned_values[...] = kvbuf[2 * head + 1].T

            def each(r, _):
                project(c, r)
                attend(q, r, 0)
                attend(q + 1, r, 1)
                return 0

            lax.fori_loop(0, row_groups, each, 0)

        return 0

    lax.fori_loop(0, heads // 2 + 1, late, 0)

    def drain(c, _):
        def each(o, _):
            @pl.when(has_up & (o <= s))
            def _():
                up_copy(c, o).wait_send()

            @pl.when(has_down & (o >= s))
            def _():
                down_copy(c, o).wait_send()

            @pl.when((o != s) & ~idle)
            def _():
                for k in range(1, groups):
                    side_copy(c, o, g, lax.rem(g + k, groups)).wait_send()

            return 0

        lax.fori_loop(0, n, each, 0)
        return 0

    lax.fori_loop(0, chunks, drain, 0)

    def kv_drain(j, _):
        def each(o, _):
            @pl.when(has_up & (o <= s))
            def _():
                kv_up_copy(j, o).wait_send()

            @pl.when(has_down & (o >= s))
            def _():
                kv_down_copy(j, o).wait_send()

            return 0

        lax.fori_loop(0, n, each, 0)

        @pl.when(host)
        def _():
            back_copy(j).wait_send()

        @pl.when(idle)
        def _():
            at = cache_ref.at[j]
            remote(at, at, back_send.at[j], back_recv.at[j], seq=partner).wait_recv()

        return 0

    lax.fori_loop(0, planes, kv_drain, 0)

    @pl.when(host)
    def _():
        for k in range(subs):
            for i in range(1, head_dev):
                x_copy(k, hx, lax.rem(hx + i, head_dev)).wait_send()
            for x in range(head_dev):
                for m in range(1, hold_dev):
                    mate_copy(k, x, hc, lax.rem(hc + m, hold_dev)).wait_send()
        for q in range(heads):
            ret_copy(q).wait_send()

    @pl.when(idle)
    def _():
        for q in range(heads):
            at = out_ref.at[q]
            remote(at, at, ret_send.at[q], ret_recv.at[q], seq=partner).wait_recv()


def local(n, groups, head_dev, hold_dev, meet_span, span_map, hidden, w_query, w_keyval, stored_kv):
    row_count, features = hidden.shape
    span_count = span_map.shape[0]
    depth, local_heads = w_query.shape[:2]
    head_width = stored_kv.shape[2] // 2
    group_size = w_query.shape[2] // head_width
    span_len = CH
    slots_dev = row_count // span_len
    planes, heads = 2 * local_heads, local_heads * group_size
    chunks = planes + heads
    offsets = jnp.arange(span_len, dtype=jnp.int32)
    key_pos = (span_map[:, None] * span_len + offsets[None, :]).reshape(-1, 1)
    key_pos = jnp.broadcast_to(key_pos, (key_pos.shape[0], head_width))
    seq_index = lax.axis_index("seq")
    guest = jnp.where(seq_index == 1, 0, n - 1)
    my_spans = jnp.concatenate(
        [
            lax.dynamic_slice_in_dim(span_map, index * slots_dev, slots_dev, 0)
            for index in (seq_index, guest)
        ]
    )
    positions = (my_spans[:, None] * span_len + offsets[None, :]).reshape(-1)
    computed_slot = (my_spans < meet_span[0]) | (my_spans == span_count - 1)
    done = jnp.repeat(computed_slot, span_len).astype(jnp.int32)[:, None]
    cosine, sine = rotary_tables(positions, head_width)
    own_kv = w_keyval.reshape(depth, planes * head_width)
    own_q = w_query.reshape(depth, heads * head_width)
    stored = stored_kv.reshape(row_count, planes, head_width).transpose(1, 0, 2)
    subs = 4
    vmem = pl.BlockSpec(memory_space=pltpu.VMEM)
    hbm = pl.BlockSpec(memory_space=pl.ANY)
    dma = pltpu.SemaphoreType.DMA
    attended, cache = pl.pallas_call(
        functools.partial(kernel, n, groups, head_dev, hold_dev, local_heads, group_size),
        out_shape=(
            jax.ShapeDtypeStruct((heads, row_count, head_width), jnp.bfloat16),
            jax.ShapeDtypeStruct((planes, row_count, head_width), jnp.bfloat16),
        ),
        in_specs=[hbm] * 4 + [vmem] * 6,
        out_specs=(vmem, vmem),
        scratch_shapes=[
            pltpu.VMEM((2 * row_count, features), jnp.bfloat16),
            pltpu.VMEM((chunks, features, head_width), jnp.bfloat16),
            pltpu.VMEM((planes, n * row_count, head_width), jnp.bfloat16),
            pltpu.VMEM((planes, 2 * row_count, head_width), jnp.bfloat16),
            pltpu.VMEM((heads, row_count, head_width), jnp.bfloat16),
            pltpu.VMEM((head_width, n * row_count), jnp.bfloat16),
            pltpu.VMEM((row_count, 2 * head_width), jnp.float32),
            dma,
            dma,
            dma((chunks,)),
        ]
        + [dma((chunks, n))] * 5
        + [dma((planes, n))] * 3
        + [dma((subs,))] * 2
        + [dma((subs, head_dev))] * 2
        + [dma((subs, head_dev, hold_dev))] * 2
        + [dma] * 2
        + [dma((planes,))] * 2
        + [dma((heads,))] * 2,
        compiler_params=pltpu.CompilerParams(
            collective_id=0, has_side_effects=True, vmem_limit_bytes=60 * 1024 * 1024
        ),
    )(hidden, own_kv, own_q, stored, cosine, sine, positions[None, :], done, done.reshape(1, -1), key_pos)
    attended = attended.transpose(1, 0, 2).reshape(row_count, local_heads, -1)
    cache = cache.transpose(1, 0, 2).reshape(row_count, local_heads, -1)
    return (attended, cache)


def solution(mesh):
    return jax.shard_map(
        functools.partial(local, *(mesh.shape[a] for a in ("seq", "grp", "head", "hold"))),
        mesh=mesh,
        in_specs=(
            P("grp"),
            P("grp"),
            P(("grp", "seq"), None),
            P("seq", ("head", "hold"), None),
            P("seq", ("head", "hold"), None),
            P(("grp", "seq"), ("head", "hold"), None),
        ),
        out_specs=(
            P(("grp", "seq"), ("head", "hold"), None),
            P(("grp", "seq"), ("head", "hold"), None),
        ),
        check_vma=False,
    )
```
